256 devices in a mesh: cam: 8 (over x_lo, y), tm: 32 (over z, x_hi, core).
Axes of the slice: x: 4 (x_hi: 2, x_lo: 2; x = x_hi * 2 + x_lo), y: 4, z: 8, core: 2. Of those that a mesh axis runs over, the one named last changes fastest.
Arguments:
- latents: bfloat16 [8, 64, 16, 32, 256], P('cam', 'tm'), may hold values from -12 to 12
- cycle_position: int32 [8], replicated, may hold values from 0 to 7, as said below
- conv_first: bfloat16 [3, 3, 3, 256, 256], replicated, may hold values from -0.078125 to 0.078125
- conv_second: bfloat16 [3, 3, 3, 256, 256], replicated, may hold values from -0.078125 to 0.078125
- norm_gain: float32 [256], replicated, may hold values from 0.5 to 1.5
- norm_shift: float32 [256], replicated, may hold values from -3 to 3
- w_query: bfloat16 [256, 256], replicated, may hold values from -8 to 8
- w_key: bfloat16 [256, 256], replicated, may hold values from -8 to 8
- w_value: bfloat16 [256, 256], replicated, may hold values from -0.375 to 0.375
- w_out: bfloat16 [256, 256], replicated, may hold values from -0.375 to 0.375
- camera_table: float32 [8, 256], replicated, may hold values from -5 to 5
- side_embed: bfloat16 [2, 256], replicated, may hold values from -5 to 5
Outputs:
- block_out: bfloat16 [8, 64, 16, 32, 256], P('cam', 'tm')
The draws below stay inside these ranges and needn't reach their ends.
Inputs may be any that keep to these rules, and one draw needn't show every extreme that they name: cycle_position[i] is the cycle place of the camera at index i of cam: the places 0 to 7 rotated, running forwards or backwards with the index, so cycle neighbours sit on neighbouring indices with wrap-around.
All inputs are finite; a program needn't handle non-finite values.
Results may differ from the reference program's by a relative error of at most 0.012.
The reference program's roundings to bfloat16 on the way (of `hidden`, `query`, `weight`, `attended` and `mixed`) count: a program that leaves them out, or rounds other values in their place, can miss the bound.
Values may be sent and summed in bfloat16 or wider, within the bound.
A program may use at most 64 MiB of HBM per device.

```python
import math
import jax
import jax.numpy as jnp
from jax import lax

C = 256
H = 16
W = 32
GROUPS = 32
CAMS = 8
FRAMES = 64


def draw_latents(key, part):
    key = jax.random.fold_in(key, 1)
    key_base = jax.random.fold_in(key, 0)
    key_chan = jax.random.fold_in(key, 1)
    key_offset = jax.random.fold_in(key, 3)
    shape = (CAMS, FRAMES, H, W, C)
    frames = jnp.arange(FRAMES, dtype=jnp.float32)
    rise = 0.5 + frames / (FRAMES - 1)
    ramp = 0.1 + 0.9 * frames / (FRAMES - 1)
    chan = jax.random.uniform(key_chan, (C,), minval=0.5, maxval=2.0)
    offset = jax.random.uniform(key_offset, (C,), minval=-1.5, maxval=1.5)
    base = jnp.clip(jax.random.normal(key_base, shape), -3.0, 3.0)
    lift = 1.5 * ramp
    values = base * rise[None, :, None, None, None] * chan + lift[None, :, None, None, None] * offset
    return values.astype(jnp.bfloat16)


def draw_w_query(key, part):
    key = jax.random.fold_in(key, 2)
    own = jnp.clip(jax.random.normal(key, (C, C)), -4.0, 4.0)
    matrix = 2.0 * own / math.sqrt(C)
    return matrix.astype(jnp.bfloat16)


def draw_w_key(key, part):
    key = jax.random.fold_in(key, 3)
    own = jnp.clip(jax.random.normal(key, (C, C)), -4.0, 4.0)
    matrix = 2.0 * own / math.sqrt(C)
    return matrix.astype(jnp.bfloat16)


def draw_cycle_position(key, part):
    key = jax.random.fold_in(key, 4)
    key_start, key_sense = jax.random.split(key)
    start = jax.random.randint(key_start, (), 0, CAMS)
    sense = 2 * jax.random.randint(key_sense, (), 0, 2) - 1
    return ((start + sense * jnp.arange(CAMS, dtype=jnp.int32)) % CAMS).astype(jnp.int32)


def gaussian(key, extent, width, bound, held_as=jnp.bfloat16):
    array = jax.random.normal(key, extent, jnp.float32) * width
    return jnp.minimum(jnp.maximum(array, -bound), bound).astype(held_as)


def setup_inputs(seed: int = 0) -> dict:
    streams_of = jax.random.split(jax.random.key(seed), 13)
    return {
        "latents": draw_latents(jax.random.fold_in(streams_of[12], 71), 0),
        "cycle_position": draw_cycle_position(jax.random.fold_in(streams_of[12], 71), 0),
        "conv_first": gaussian(streams_of[2], (3, 3, 3, C, C), (27 * C) ** -0.5, 0.078125),
        "conv_second": gaussian(streams_of[3], (3, 3, 3, C, C), (27 * C) ** -0.5, 0.078125),
        "norm_gain": jnp.clip(jax.random.uniform(streams_of[4], (C,), jnp.float32, 0.5, 1.5), 0.5, 1.5),
        "norm_shift": gaussian(streams_of[5], (C,), 0.5, 3.0, jnp.float32),
        "w_query": draw_w_query(jax.random.fold_in(streams_of[12], 71), 0),
        "w_key": draw_w_key(jax.random.fold_in(streams_of[12], 71), 0),
        "w_value": gaussian(streams_of[8], (C, C), C ** -0.5, 0.375),
        "w_out": gaussian(streams_of[9], (C, C), C ** -0.5, 0.375),
        "camera_table": gaussian(streams_of[10], (CAMS, C), 1.0, 5.0, jnp.float32),
        "side_embed": gaussian(streams_of[11], (2, C), 1.0, 5.0),
    }


def causal_conv(frames, past, kernel):
    count, rows, cols, chans = frames.shape
    full = jnp.concatenate([past, frames], axis=0)
    full = jnp.pad(full, ((0, 0), (1, 1), (1, 1), (0, 0)))
    total = jnp.zeros((count * rows * cols, kernel.shape[-1]), jnp.float32)
    for step_t in range(3):
        for step_r in range(3):
            for step_c in range(3):
                tap = full[step_t:step_t + count, step_r:step_r + rows, step_c:step_c + cols].reshape(-1, chans)
                total = total + jnp.dot(tap, kernel[step_t, step_r, step_c], preferred_element_type=jnp.float32)
    return total.reshape(count, rows, cols, -1)

def attend_frame(query, keys, values, side_terms):
    half = keys.shape[0] // 2
    raw = jnp.einsum('qc,kc->qk', query.astype(jnp.float32), keys.astype(jnp.float32))
    bias = jnp.concatenate([jnp.broadcast_to(side_terms[:, 0:1], (query.shape[0], half)), jnp.broadcast_to(side_terms[:, 1:2], (query.shape[0], half))], axis=1)
    scores = (raw + bias) * C ** (-0.5)
    top = lax.optimization_barrier(jnp.max(scores, axis=1, keepdims=True))
    expo = jnp.exp(scores - top)
    weight = (expo / lax.optimization_barrier(jnp.sum(expo, axis=1, keepdims=True))).astype(jnp.bfloat16)
    return jnp.dot(weight, values, preferred_element_type=jnp.float32).astype(jnp.bfloat16)

def reference(latents, cycle_position, conv_first, conv_second, norm_gain, norm_shift, w_query, w_key, w_value, w_out, camera_table, side_embed):

    def first_section(frames):
        past = jnp.concatenate([frames[0:1], frames[0:1]], axis=0)
        first = causal_conv(frames, past, conv_first)
        grouped = first.reshape(FRAMES, H, W, GROUPS, C // GROUPS)
        mean = lax.optimization_barrier(jnp.mean(grouped, axis=(0, 1, 2, 4), keepdims=True))
        dev = grouped - mean
        spread = lax.optimization_barrier(jnp.mean(dev * dev, axis=(0, 1, 2, 4), keepdims=True))
        normed = (dev * lax.rsqrt(spread + 1e-05)).reshape(FRAMES, H, W, C) * norm_gain + norm_shift
        return jax.nn.silu(normed).astype(jnp.bfloat16)
    hidden_all = lax.map(first_section, latents)

    def second_section(camera):
        place = cycle_position[camera]
        left_idx = jnp.argmax((cycle_position == (place - 1) % CAMS).astype(jnp.int32)).astype(jnp.int32)
        right_idx = jnp.argmax((cycle_position == (place + 1) % CAMS).astype(jnp.int32)).astype(jnp.int32)
        hidden = hidden_all[camera]
        rows = hidden.reshape(-1, C)
        table_row = camera_table[place]
        extra = jnp.dot(table_row, w_query.astype(jnp.float32), precision=lax.Precision.HIGHEST)
        query = (jnp.dot(rows, w_query, preferred_element_type=jnp.float32) + extra).astype(jnp.bfloat16)
        left_rows = hidden_all[left_idx].reshape(-1, C)
        right_rows = hidden_all[right_idx].reshape(-1, C)
        keys_left = jnp.dot(left_rows, w_key, preferred_element_type=jnp.float32).astype(jnp.bfloat16)
        values_left = jnp.dot(left_rows, w_value, preferred_element_type=jnp.float32).astype(jnp.bfloat16)
        keys_right = jnp.dot(right_rows, w_key, preferred_element_type=jnp.float32).astype(jnp.bfloat16)
        values_right = jnp.dot(right_rows, w_value, preferred_element_type=jnp.float32).astype(jnp.bfloat16)
        side_terms = jnp.dot(query, side_embed.T, preferred_element_type=jnp.float32)
        cells = H * W
        keys = jnp.concatenate([keys_left.reshape(FRAMES, cells, C), keys_right.reshape(FRAMES, cells, C)], axis=1)
        values = jnp.concatenate([values_left.reshape(FRAMES, cells, C), values_right.reshape(FRAMES, cells, C)], axis=1)
        attended = lax.map(lambda items: attend_frame(*items), (query.reshape(FRAMES, cells, C), keys, values, side_terms.reshape(FRAMES, cells, 2)))
        out_proj = jnp.dot(attended.reshape(-1, C), w_out, preferred_element_type=jnp.float32)
        mixed = (rows.astype(jnp.float32) + out_proj).astype(jnp.bfloat16).reshape(FRAMES, H, W, C)
        past = jnp.concatenate([mixed[0:1], mixed[0:1]], axis=0)
        second = causal_conv(mixed, past, conv_second)
        return (latents[camera].astype(jnp.float32) + second).astype(jnp.bfloat16)
    return lax.map(second_section, jnp.arange(CAMS, dtype=jnp.int32))
```

```python
import functools

import jax
import jax.numpy as jnp
from jax import lax
from jax.experimental import pallas as pl
from jax.experimental.pallas import tpu as pltpu
from jax.sharding import PartitionSpec as P

GROUPS = 32
F32 = jnp.float32
BF16 = jnp.bfloat16
MESH = pl.DeviceIdType.MESH
ROWS, COLS, CHANS = 16, 32, 256
CELLS = ROWS * COLS
TALL = CELLS + 2 * COLS


def dot(a, b):
    return jnp.dot(a, b, preferred_element_type=F32)


def dot_t(a, b):
    return lax.dot_general(a, b, (((1,), (1,)), ((), ())), preferred_element_type=F32)


def conv_terms(buf, w, terms):
    parts = []
    for ds in range(3):
        acc = jnp.zeros((CELLS, CHANS), F32)
        for slot, dt in terms:
            for dr in range(3):
                acc += dot(
                    buf[slot, pl.ds(dr * COLS, CELLS), :],
                    w[dt * 3 + dr, pl.ds(ds * CHANS, CHANS), :],
                )
        parts.append(acc)
    col = lax.rem(lax.broadcasted_iota(jnp.int32, (CELLS, CHANS), 0), COLS)
    left = jnp.where(col == 0, 0.0, pltpu.roll(parts[0], 1, 0))
    right = jnp.where(col == COLS - 1, 0.0, pltpu.roll(parts[2], CELLS - 1, 0))
    return parts[1] + left + right


def block_kernel(
    cams,
    tms,
    lat_ref,
    place_ref,
    w1_ref,
    w2_ref,
    gain_ref,
    shift_ref,
    wq_ref,
    wk_ref,
    wv_ref,
    wo_ref,
    table_ref,
    side_ref,
    out_ref,
    xb,
    mb,
    w1,
    w2,
    first,
    part,
    far,
    nbr,
    hid,
    query,
    st,
    fw,
    fw_in,
    place,
    gain,
    shift,
    wq,
    wk,
    wv,
    wo,
    table,
    side,
    lsem,
    hsend,
    hrecv,
    ssend,
    srecv,
    csend,
    crecv,
    fsend,
    frecv,
    msend,
    mrecv,
):
    cam = lax.axis_index("cam")
    tm = lax.axis_index("tm")
    cam_above = lax.rem(cam + 1, cams)
    cam_below = lax.rem(cam + cams - 1, cams)
    core = lax.rem(tm, 2)
    pair = tm + 1 - 2 * core
    after = (cam, lax.rem(tm + 1, tms))
    is_first = tm == 0
    is_last = tm == tms - 1

    def later(i):
        return (cam, lax.rem(tm + i, tms))

    def remote(src, dst, send, recv, to):
        return pltpu.make_async_remote_copy(
            src_ref=src,
            dst_ref=dst,
            send_sem=send,
            recv_sem=recv,
            device_id=to,
            device_id_type=MESH,
        )

    inner = pl.ds(COLS, CELLS)
    half = [pl.ds(f * CELLS, CELLS) for f in range(2)]
    plane = [pl.ds(3 * dt, 3) for dt in range(3)]

    moves = (
        [(lat_ref.at[half[f]], xb.at[2 + f, inner]) for f in (1, 0)]
        + [(w1_ref.at[plane[dt]], w1.at[plane[dt]]) for dt in (2, 1, 0)]
        + [
            (place_ref, place),
            (table_ref, table),
            (side_ref, side),
            (gain_ref, gain),
            (shift_ref, shift),
            (wq_ref, wq),
            (wk_ref, wk),
            (wv_ref, wv),
            (wo_ref, wo),
            (w2_ref, w2),
        ]
    )
    loads = [pltpu.make_async_copy(src, dst, lsem.at[i]) for i, (src, dst) in enumerate(moves)]
    for copy in loads[:5]:
        copy.start()

    barrier = pltpu.get_barrier_semaphore()
    greeted = [later(tms - 1), later(1)]
    greeted += [(c, t) for c in (cam_above, cam_below) for t in (tm, pair)]
    greeted += [later(i) for i in range(2, tms - 1)]
    if tms == 2:
        greeted = greeted[1:]
    for to in greeted:
        pl.semaphore_signal(barrier, inc=1, device_id=to, device_id_type=MESH)
    pl.semaphore_wait(barrier, len(greeted))

    halo = [
        remote(lat_ref.at[half[f]], xb.at[f, inner], hsend.at[f], hrecv.at[f], after)
        for f in range(2)
    ]

    @pl.when(jnp.logical_not(is_last))
    def _():
        halo[1].start()
        halo[0].start()

    for copy in loads[5:]:
        copy.start()
    zero = jnp.zeros((COLS, CHANS), BF16)
    for slot in range(4):
        for at in (0, COLS + CELLS):
            xb[slot, pl.ds(at, COLS), :] = zero
            mb[slot, pl.ds(at, COLS), :] = zero
    for copy in loads[:3]:
        copy.wait()
    first[half[0], :] = conv_terms(xb, w1, [(2, 2)])
    loads[3].wait()
    first[half[1], :] = conv_terms(xb, w1, [(3, 2), (2, 1)])
    loads[4].wait()

    @pl.when(is_first)
    def _():
        xb[0, inner, :] = xb[2, inner, :]
        xb[1, inner, :] = xb[2, inner, :]

    @pl.when(jnp.logical_not(is_first))
    def _():
        halo[1].wait_recv()

    first[half[1], :] += conv_terms(xb, w1, [(1, 0)])

    means, squares = [None, None], [None, None]

    def measure(f):
        rows = first[half[f], :]
        means[f] = jnp.sum(rows, axis=0, keepdims=True) / CELLS
        dev = rows - means[f]
        squares[f] = jnp.sum(dev * dev, axis=0, keepdims=True)

    measure(1)

    @pl.when(jnp.logical_not(is_first))
    def _():
        halo[0].wait_recv()

    first[half[0], :] += conv_terms(xb, w1, [(0, 0), (1, 1)])
    measure(0)

    mean_here = 0.5 * (means[0] + means[1])
    gap = means[1] - means[0]
    st[0, 0:1, :] = mean_here
    st[0, 1:2, :] = squares[0] + squares[1] + (0.5 * CELLS) * (gap * gap)
    swaps = [
        remote(st.at[0], st.at[i], ssend.at[i - 1], srecv.at[i - 1], later(i))
        for i in range(1, tms)
    ]
    for copy in swaps:
        copy.start()

    sides_of = (cam_above, cam_below)
    early = [
        [
            remote(
                first.at[half[f]],
                far.at[n, half[f]],
                csend.at[2 * f + n],
                crecv.at[2 * f + n],
                (sides_of[n], tm),
            )
            for n in range(2)
        ]
        for f in range(2)
    ]
    late = [
        [
            remote(
                hid.at[half[f]],
                nbr.at[n, half[f]],
                csend.at[2 * f + n],
                crecv.at[2 * f + n],
                (sides_of[n], tm),
            )
            for n in range(2)
        ]
        for f in range(2)
    ]

    @pl.when(core == 1)
    def _():
        for f in (1, 0):
            for copy in early[f]:
                copy.start()

    row_group = lax.broadcasted_iota(jnp.int32, (CHANS, CHANS), 0) // (CHANS // GROUPS)
    col_group = lax.broadcasted_iota(jnp.int32, (CHANS, CHANS), 1) // (CHANS // GROUPS)
    same = (row_group == col_group).astype(F32)

    def group_sum(row):
        wide = jnp.broadcast_to(row, (8, CHANS))
        return jnp.dot(
            wide, same, precision=lax.Precision.HIGHEST, preferred_element_type=F32
        )[0:1]

    for copy in loads[5:]:
        copy.wait()
    ids = lax.broadcasted_iota(jnp.int32, (cams, CHANS), 0)
    my_place = place[cam]
    below_place = place[cam_below]
    below_is_left = below_place == lax.rem(my_place + cams - 1, cams)
    table_row = jnp.sum(jnp.where(ids == my_place, table[...], 0.0), axis=0, keepdims=True)
    extra = jnp.dot(
        jnp.broadcast_to(table_row, (8, CHANS)),
        wq[...].astype(F32),
        precision=lax.Precision.HIGHEST,
        preferred_element_type=F32,
    )[0:1]
    sides = side[...].astype(F32)
    side_below = jnp.where(below_is_left, sides[0:1], sides[1:2])
    side_above = jnp.where(below_is_left, sides[1:2], sides[0:1])
    side_wide = jnp.concatenate(
        [
            jnp.broadcast_to(side_below, (128, CHANS)),
            jnp.broadcast_to(side_above, (128, CHANS)),
        ],
        axis=0,
    ).astype(BF16)

    for copy in swaps:
        copy.wait()
    cells = 2 * CELLS
    every = st[:, 0, :]
    mean_chan = jnp.sum(every, axis=0, keepdims=True) / tms
    away = every - mean_chan
    m2_chan = jnp.sum(st[:, 1, :], axis=0, keepdims=True) + cells * jnp.sum(
        away * away, axis=0, keepdims=True
    )
    per_group = CHANS // GROUPS
    mean = group_sum(mean_chan) / per_group
    away = mean_chan - mean
    spread = group_sum(m2_chan + (cells * tms) * (away * away)) / (per_group * cells * tms)
    scale = lax.rsqrt(spread + 1e-05) * gain[...]
    fw[0:1, :] = mean
    fw[1:2, :] = scale
    forwards = [
        remote(fw, fw_in.at[n], fsend.at[n], frecv.at[n], (sides_of[n], pair)) for n in range(2)
    ]

    @pl.when(core == 0)
    def _():
        for copy in forwards:
            copy.start()

    def silu(v):
        return (v / (1.0 + jnp.exp(-v))).astype(BF16)

    for f in (1, 0):
        hid[half[f], :] = silu((first[half[f], :] - mean) * scale + shift[...])

        @pl.when(core == 0)
        def _():
            for copy in late[f]:
                copy.start()

    for f in (1, 0):
        query[half[f], :] = (dot(hid[half[f], :], wq[...]) + extra).astype(BF16)

    mixed_halo = [
        remote(mb.at[2 + f, inner], mb.at[f, inner], msend.at[f], mrecv.at[f], after)
        for f in range(2)
    ]

    @pl.when(core == 1)
    def _():
        for copy in forwards:
            copy.wait_recv()

    for f in (1, 0):
        q = query[half[f], :]
        tilt = dot_t(q, side_wide)
        bias = [tilt[:, 0:1], tilt[:, 128:129]]
        scores, values = [], []

        @pl.when(core == 1)
        def _():
            for n in range(2):
                early[f][n].wait_recv()
                nbr[n, half[f], :] = silu(
                    (far[n, half[f], :] - fw_in[n, 0:1, :]) * fw_in[n, 1:2, :] + shift[...]
                )

        @pl.when(core == 0)
        def _():
            for n in range(2):
                late[f][n].wait_recv()

        for n in range(2):
            rows = nbr[n, half[f], :]
            keys = dot(rows, wk[...]).astype(BF16)
            values.append(dot(rows, wv[...]).astype(BF16))
            scores.append((dot_t(q, keys) + bias[n]) * CHANS ** (-0.5))
        top = jnp.maximum(
            jnp.max(scores[0], axis=1, keepdims=True), jnp.max(scores[1], axis=1, keepdims=True)
        )
        expo = [jnp.exp(s - top) for s in scores]
        total = jnp.sum(expo[0], axis=1, keepdims=True) + jnp.sum(expo[1], axis=1, keepdims=True)
        inverse = 1.0 / total
        attended = (
            dot((expo[0] * inverse).astype(BF16), values[0])
            + dot((expo[1] * inverse).astype(BF16), values[1])
        ).astype(BF16)
        mixed = hid[half[f], :].astype(F32) + dot(attended, wo[...])
        mb[2 + f, inner, :] = mixed.astype(BF16)

        @pl.when(jnp.logical_not(is_last))
        def _():
            mixed_halo[f].start()

    part[half[0], :] = conv_terms(mb, w2, [(2, 2)])
    part[half[1], :] = conv_terms(mb, w2, [(3, 2), (2, 1)])

    @pl.when(is_first)
    def _():
        mb[0, inner, :] = mb[2, inner, :]
        mb[1, inner, :] = mb[2, inner, :]

    @pl.when(jnp.logical_not(is_first))
    def _():
        mixed_halo[1].wait_recv()

    total = part[half[1], :] + conv_terms(mb, w2, [(1, 0)])
    out_ref[half[1], :] = (xb[3, inner, :].astype(F32) + total).astype(BF16)

    @pl.when(jnp.logical_not(is_first))
    def _():
        mixed_halo[0].wait_recv()

    total = part[half[0], :] + conv_terms(mb, w2, [(0, 0), (1, 1)])
    out_ref[half[0], :] = (xb[2, inner, :].astype(F32) + total).astype(BF16)

    @pl.when(core == 1)
    def _():
        for f in range(2):
            for copy in early[f]:
                copy.wait_send()

    @pl.when(core == 0)
    def _():
        for f in range(2):
            for copy in late[f]:
                copy.wait_send()
        for copy in forwards:
            copy.wait_send()

    @pl.when(jnp.logical_not(is_last))
    def _():
        for f in range(2):
            halo[f].wait_send()
            mixed_halo[f].wait_send()


def on_device(
    latents,
    cycle_position,
    conv_first,
    conv_second,
    norm_gain,
    norm_shift,
    w_query,
    w_key,
    w_value,
    w_out,
    camera_table,
    side_embed,
):
    cams, tms = lax.axis_size("cam"), lax.axis_size("tm")
    shape = latents.shape
    vmem = pl.BlockSpec(memory_space=pltpu.VMEM)
    hbm = pl.BlockSpec(memory_space=pltpu.HBM)
    dma = pltpu.SemaphoreType.DMA
    flops = 2 * 1024 * 256 * 256 * (54 + 6) + 4 * 1024 * 1024 * 256
    out = pl.pallas_call(
        functools.partial(block_kernel, cams, tms),
        out_shape=jax.ShapeDtypeStruct((2 * CELLS, CHANS), BF16),
        in_specs=[hbm] * 12,
        out_specs=vmem,
        scratch_shapes=[
            pltpu.VMEM((4, TALL, CHANS), BF16),
            pltpu.VMEM((4, TALL, CHANS), BF16),
            pltpu.VMEM((9, 3 * CHANS, CHANS), BF16),
            pltpu.VMEM((9, 3 * CHANS, CHANS), BF16),
            pltpu.VMEM((2 * CELLS, CHANS), F32),
            pltpu.VMEM((2 * CELLS, CHANS), F32),
            pltpu.VMEM((2, 2 * CELLS, CHANS), F32),
            pltpu.VMEM((2, 2 * CELLS, CHANS), BF16),
            pltpu.VMEM((2 * CELLS, CHANS), BF16),
            pltpu.VMEM((2 * CELLS, CHANS), BF16),
            pltpu.VMEM((tms, 2, CHANS), F32),
            pltpu.VMEM((2, CHANS), F32),
            pltpu.VMEM((2, 2, CHANS), F32),
            pltpu.SMEM((cams,), jnp.int32),
            pltpu.VMEM((1, CHANS), F32),
            pltpu.VMEM((1, CHANS), F32),
        ]
        + [pltpu.VMEM((CHANS, CHANS), BF16)] * 4
        + [
            pltpu.VMEM((cams, CHANS), F32),
            pltpu.VMEM((2, CHANS), BF16),
            dma((15,)),
            dma((2,)),
            dma((2,)),
            dma((tms - 1,)),
            dma((tms - 1,)),
            dma((4,)),
            dma((4,)),
            dma((2,)),
            dma((2,)),
            dma((2,)),
            dma((2,)),
        ],
        compiler_params=pltpu.CompilerParams(
            collective_id=0, has_side_effects=True, vmem_limit_bytes=62 * 2**20
        ),
        cost_estimate=pl.CostEstimate(
            flops=flops, bytes_accessed=9 * 2**20, transcendentals=2**20
        ),
    )(
        latents.reshape(2 * CELLS, CHANS),
        cycle_position,
        conv_first.reshape(9, 3 * CHANS, CHANS),
        conv_second.reshape(9, 3 * CHANS, CHANS),
        norm_gain.reshape(1, CHANS),
        norm_shift.reshape(1, CHANS),
        w_query,
        w_key,
        w_value,
        w_out,
        camera_table,
        side_embed,
    )
    return out.reshape(shape)


def solution(mesh):
    in_specs = (P("cam", "tm", None, None, None),) + (P(),) * 11
    out_specs = P("cam", "tm", None, None, None)
    return jax.shard_map(
        on_device, mesh=mesh, in_specs=in_specs, out_specs=out_specs, check_vma=False
    )
```

```python
import functools

import jax
import jax.numpy as jnp
from jax import lax
from jax.experimental import pallas as pl
from jax.experimental.pallas import tpu as pltpu
from jax.sharding import PartitionSpec as P

GROUPS = 32
F32 = jnp.float32
BF16 = jnp.bfloat16
MESH = pl.DeviceIdType.MESH
ROWS, COLS, CHANS = 16, 32, 256
CELLS = ROWS * COLS
TALL = CELLS + 2 * COLS
SPLIT = 256


def dot(a, b):
    return jnp.dot(a, b, preferred_element_type=F32)


def dot_t(a, b):
    return lax.dot_general(a, b, (((1,), (1,)), ((), ())), preferred_element_type=F32)


def conv_terms(buf, w, terms):
    parts = []
    for ds in range(3):
        acc = jnp.zeros((CELLS, CHANS), F32)
        for slot, dt in terms:
            for dr in range(3):
                acc += dot(
                    buf[slot, pl.ds(dr * COLS, CELLS), :],
                    w[dt * 3 + dr, pl.ds(ds * CHANS, CHANS), :],
                )
        parts.append(acc)
    col = lax.rem(lax.broadcasted_iota(jnp.int32, (CELLS, CHANS), 0), COLS)
    left = jnp.where(col == 0, 0.0, pltpu.roll(parts[0], 1, 0))
    right = jnp.where(col == COLS - 1, 0.0, pltpu.roll(parts[2], CELLS - 1, 0))
    return parts[1] + left + right


def block_kernel(
    cams,
    tms,
    lat_ref,
    place_ref,
    w1_ref,
    w2_ref,
    gain_ref,
    shift_ref,
    wq_ref,
    wk_ref,
    wv_ref,
    wo_ref,
    table_ref,
    side_ref,
    out_ref,
    xb,
    mb,
    w1,
    w2,
    first,
    part,
    far,
    nbr,
    hid,
    query,
    own,
    mate,
    st,
    fw,
    fw_in,
    place,
    gain,
    shift,
    wq,
    wk,
    wv,
    wo,
    table,
    side,
    lsem,
    hsend,
    hrecv,
    psem,
    ssend,
    srecv,
    csend,
    crecv,
    fsend,
    frecv,
    msend,
    mrecv,
):
    cam = lax.axis_index("cam")
    tm = lax.axis_index("tm")
    cam_above = lax.rem(cam + 1, cams)
    cam_below = lax.rem(cam + cams - 1, cams)
    core = lax.rem(tm, 2)
    pair = tm + 1 - 2 * core
    after = (cam, lax.rem(tm + 1, tms))
    sides_of = (cam_above, cam_below)
    chips = tms // 2
    is_first = tm == 0
    is_last = tm == tms - 1

    def later(i):
        return (cam, lax.rem(tm + i, tms))

    def remote(src, dst, send, recv, to):
        return pltpu.make_async_remote_copy(
            src_ref=src,
            dst_ref=dst,
            send_sem=send,
            recv_sem=recv,
            device_id=to,
            device_id_type=MESH,
        )

    inner = pl.ds(COLS, CELLS)
    half = [pl.ds(f * CELLS, CELLS) for f in range(2)]
    plane = [pl.ds(3 * dt, 3) for dt in range(3)]

    moves = (
        [(lat_ref.at[half[f]], xb.at[2 + f, inner]) for f in (1, 0)]
        + [(w1_ref.at[plane[dt]], w1.at[plane[dt]]) for dt in (2, 1, 0)]
        + [
            (place_ref, place),
            (table_ref, table),
            (side_ref, side),
            (gain_ref, gain),
            (shift_ref, shift),
            (wq_ref, wq),
            (wk_ref, wk),
            (wv_ref, wv),
            (wo_ref, wo),
            (w2_ref, w2),
        ]
    )
    loads = [pltpu.make_async_copy(src, dst, lsem.at[i]) for i, (src, dst) in enumerate(moves)]
    for copy in loads[:5]:
        copy.start()

    barrier = pltpu.get_barrier_semaphore()

    def greet(to):
        pl.semaphore_signal(barrier, inc=1, device_id=to, device_id_type=MESH)

    halo = [
        remote(lat_ref.at[half[f]], xb.at[f, inner], hsend.at[f], hrecv.at[f], after)
        for f in range(2)
    ]

    @pl.when(core == 0)
    def _():
        greet(later(tms - 1))
        greet((cam, pair))
        for c in sides_of:
            greet((c, tm))
        for i in range(1, chips):
            greet(later(2 * i))
        pl.semaphore_wait(barrier, tms + 1)

    @pl.when(core == 1)
    def _():
        greet((cam, pair))
        for c in sides_of:
            greet((c, tm))
        pl.semaphore_wait(barrier, 4)

    @pl.when(jnp.logical_not(is_last))
    def _():
        halo[1].start()
        halo[0].start()

    @pl.when(core == 1)
    def _():
        for i in range(1, chips):
            greet(later(2 * i + tms - 1))

    for copy in loads[5:]:
        copy.start()
    zero = jnp.zeros((COLS, CHANS), BF16)
    for slot in range(4):
        for at in (0, COLS + CELLS):
            xb[slot, pl.ds(at, COLS), :] = zero
            mb[slot, pl.ds(at, COLS), :] = zero
    for copy in loads[:3]:
        copy.wait()
    first[half[0], :] = conv_terms(xb, w1, [(2, 2)])
    loads[3].wait()
    first[half[1], :] = conv_terms(xb, w1, [(3, 2), (2, 1)])
    loads[4].wait()

    @pl.when(is_first)
    def _():
        xb[0, inner, :] = xb[2, inner, :]
        xb[1, inner, :] = xb[2, inner, :]

    @pl.when(jnp.logical_not(is_first))
    def _():
        halo[1].wait_recv()

    first[half[1], :] += conv_terms(xb, w1, [(1, 0)])

    means, squares = [None, None], [None, None]

    def measure(f):
        rows = first[half[f], :]
        means[f] = jnp.sum(rows, axis=0, keepdims=True) / CELLS
        dev = rows - means[f]
        squares[f] = jnp.sum(dev * dev, axis=0, keepdims=True)

    measure(1)

    early = [
        [
            remote(
                first.at[rows],
                far.at[n, pl.ds(at, size)],
                csend.at[2 * i + n],
                crecv.at[2 * i + n],
                (sides_of[n], tm),
            )
            for n in range(2)
        ]
        for i, (at, size, rows) in enumerate(
            (at, size, pl.ds(CELLS + at, size)) for at, size in ((0, SPLIT), (SPLIT, CELLS - SPLIT))
        )
    ]

    @pl.when(core == 0)
    def _():
        for copy in early[0]:
            copy.start()

    @pl.when(jnp.logical_not(is_first))
    def _():
        halo[0].wait_recv()

    first[half[0], :] += conv_terms(xb, w1, [(0, 0), (1, 1)])
    measure(0)

    def joined(mean_a, mean_b, square_a, square_b, count):
        gap = mean_b - mean_a
        return 0.5 * (mean_a + mean_b), square_a + square_b + (0.5 * count) * (gap * gap)

    mean_here, square_here = joined(means[0], means[1], squares[0], squares[1], CELLS)
    hand = remote(own, mate, psem.at[0], psem.at[1], (cam, pair))
    own[0:1, :] = mean_here
    own[1:2, :] = square_here
    swaps = [remote(st.at[0], st.at[0], ssend.at[0], srecv.at[0], (cam, pair))]
    for i in range(1, chips):
        swaps.append(remote(st.at[0], st.at[i], ssend.at[2 * i], srecv.at[i], later(2 * i)))
    for i in range(1, chips):
        swaps.append(remote(st.at[0], st.at[i], ssend.at[2 * i + 1], srecv.at[i], later(2 * i + 1)))

    @pl.when(core == 0)
    def _():
        hand.wait_recv()
        mean_chip, square_chip = joined(
            mean_here, mate[0:1, :], square_here, mate[1:2, :], 2 * CELLS
        )
        st[0, 0:1, :] = mean_chip
        st[0, 1:2, :] = square_chip
        for copy in swaps:
            copy.start()
        for copy in early[1]:
            copy.start()

    @pl.when(core == 1)
    def _():
        hand.start()
        for pieces in early:
            for copy in pieces:
                copy.start()

    lane = lax.broadcasted_iota(jnp.int32, (8, CHANS), 1)

    def group_sum(row):
        wide = jnp.broadcast_to(row, (8, CHANS))
        for bit in (1, 2, 4):
            wide += jnp.where(
                lane & bit == 0, pltpu.roll(wide, CHANS - bit, 1), pltpu.roll(wide, bit, 1)
            )
        return wide[0:1]

    for copy in loads[5:]:
        copy.wait()
    ids = lax.broadcasted_iota(jnp.int32, (cams, CHANS), 0)
    my_place = place[cam]
    below_place = place[cam_below]
    below_is_left = below_place == lax.rem(my_place + cams - 1, cams)
    table_row = jnp.sum(jnp.where(ids == my_place, table[...], 0.0), axis=0, keepdims=True)
    extra = jnp.dot(
        jnp.broadcast_to(table_row, (8, CHANS)),
        wq[...].astype(F32),
        precision=lax.Precision.HIGHEST,
        preferred_element_type=F32,
    )[0:1]
    sides = side[...].astype(F32)
    side_below = jnp.where(below_is_left, sides[0:1], sides[1:2])
    side_above = jnp.where(below_is_left, sides[1:2], sides[0:1])
    side_wide = jnp.concatenate(
        [
            jnp.broadcast_to(side_below, (128, CHANS)),
            jnp.broadcast_to(side_above, (128, CHANS)),
        ],
        axis=0,
    ).astype(BF16)

    @pl.when(core == 1)
    def _():
        swaps[0].wait_recv()

    for copy in swaps[1:chips]:
        copy.wait_recv()
    cells = 4 * CELLS
    every = st[:, 0, :]
    mean_chan = jnp.sum(every, axis=0, keepdims=True) / chips
    away = every - mean_chan
    m2_chan = jnp.sum(st[:, 1, :], axis=0, keepdims=True) + cells * jnp.sum(
        away * away, axis=0, keepdims=True
    )
    per_group = CHANS // GROUPS
    mean = group_sum(mean_chan) / per_group
    away = mean_chan - mean
    spread = group_sum(m2_chan + (cells * chips) * (away * away)) / (
        per_group * cells * chips
    )
    scale = lax.rsqrt(spread + 1e-05) * gain[...]
    fw[0:1, :] = mean
    fw[1:2, :] = scale
    forwards = [
        remote(fw, fw_in.at[n], fsend.at[n], frecv.at[n], (sides_of[n], tm)) for n in range(2)
    ]
    for copy in forwards:
        copy.start()

    def silu(v):
        return (v / (1.0 + jnp.exp(-v))).astype(BF16)

    late = [
        remote(hid.at[half[0]], nbr.at[n], csend.at[4 + n], crecv.at[4 + n], (sides_of[n], tm))
        for n in range(2)
    ]
    for f in range(2):
        hid[half[f], :] = silu((first[half[f], :] - mean) * scale + shift[...])
        if f == 0:
            for copy in late:
                copy.start()
    for f in (1, 0):
        query[half[f], :] = (dot(hid[half[f], :], wq[...]) + extra).astype(BF16)

    mixed_halo = [
        remote(mb.at[2 + f, inner], mb.at[f, inner], msend.at[f], mrecv.at[f], after)
        for f in range(2)
    ]

    for copy in forwards:
        copy.wait_recv()

    for f in (1, 0):
        q = query[half[f], :]
        tilt = dot_t(q, side_wide)
        bias = [tilt[:, 0:1], tilt[:, 128:129]]
        scores, values = [], []

        for n in range(2):
            if f == 1:
                early[0][n].wait_recv()
                early[1][n].wait_recv()
                rows = silu((far[n] - fw_in[n, 0:1, :]) * fw_in[n, 1:2, :] + shift[...])
            else:
                late[n].wait_recv()
                rows = nbr[n]
            keys = dot(rows, wk[...]).astype(BF16)
            values.append(dot(rows, wv[...]).astype(BF16))
            scores.append((dot_t(q, keys) + bias[n]) * CHANS ** (-0.5))
        top = jnp.maximum(
            jnp.max(scores[0], axis=1, keepdims=True), jnp.max(scores[1], axis=1, keepdims=True)
        )
        expo = [jnp.exp(s - top) for s in scores]
        total = jnp.sum(expo[0], axis=1, keepdims=True) + jnp.sum(expo[1], axis=1, keepdims=True)
        inverse = 1.0 / total
        attended = (
            dot((expo[0] * inverse).astype(BF16), values[0])
            + dot((expo[1] * inverse).astype(BF16), values[1])
        ).astype(BF16)
        mixed = hid[half[f], :].astype(F32) + dot(attended, wo[...])
        mb[2 + f, inner, :] = mixed.astype(BF16)

        @pl.when(jnp.logical_not(is_last))
        def _():
            mixed_halo[f].start()

    part[half[0], :] = conv_terms(mb, w2, [(2, 2)])
    part[half[1], :] = conv_terms(mb, w2, [(3, 2), (2, 1)])

    @pl.when(is_first)
    def _():
        mb[0, inner, :] = mb[2, inner, :]
        mb[1, inner, :] = mb[2, inner, :]

    @pl.when(jnp.logical_not(is_first))
    def _():
        mixed_halo[1].wait_recv()

    total = part[half[1], :] + conv_terms(mb, w2, [(1, 0)])
    out_ref[half[1], :] = (xb[3, inner, :].astype(F32) + total).astype(BF16)

    @pl.when(jnp.logical_not(is_first))
    def _():
        mixed_halo[0].wait_recv()

    total = part[half[0], :] + conv_terms(mb, w2, [(0, 0), (1, 1)])
    out_ref[half[0], :] = (xb[2, inner, :].astype(F32) + total).astype(BF16)

    for copy in early[0] + early[1] + late + forwards:
        copy.wait_send()

    @pl.when(core == 0)
    def _():
        for copy in swaps:
            copy.wait_send()

    @pl.when(core == 1)
    def _():
        hand.wait_send()

    @pl.when(jnp.logical_not(is_last))
    def _():
        for f in range(2):
            halo[f].wait_send()
            mixed_halo[f].wait_send()


def on_device(
    latents,
    cycle_position,
    conv_first,
    conv_second,
    norm_gain,
    norm_shift,
    w_query,
    w_key,
    w_value,
    w_out,
    camera_table,
    side_embed,
):
    cams, tms = lax.axis_size("cam"), lax.axis_size("tm")
    shape = latents.shape
    vmem = pl.BlockSpec(memory_space=pltpu.VMEM)
    hbm = pl.BlockSpec(memory_space=pltpu.HBM)
    dma = pltpu.SemaphoreType.DMA
    flops = 2 * 1024 * 256 * 256 * (54 + 6) + 4 * 1024 * 1024 * 256
    out = pl.pallas_call(
        functools.partial(block_kernel, cams, tms),
        out_shape=jax.ShapeDtypeStruct((2 * CELLS, CHANS), BF16),
        in_specs=[hbm] * 12,
        out_specs=vmem,
        scratch_shapes=[
            pltpu.VMEM((4, TALL, CHANS), BF16),
            pltpu.VMEM((4, TALL, CHANS), BF16),
            pltpu.VMEM((9, 3 * CHANS, CHANS), BF16),
            pltpu.VMEM((9, 3 * CHANS, CHANS), BF16),
            pltpu.VMEM((2 * CELLS, CHANS), F32),
            pltpu.VMEM((2 * CELLS, CHANS), F32),
            pltpu.VMEM((2, CELLS, CHANS), F32),
            pltpu.VMEM((2, CELLS, CHANS), BF16),
            pltpu.VMEM((2 * CELLS, CHANS), BF16),
            pltpu.VMEM((2 * CELLS, CHANS), BF16),
            pltpu.VMEM((2, CHANS), F32),
            pltpu.VMEM((2, CHANS), F32),
            pltpu.VMEM((tms // 2, 2, CHANS), F32),
            pltpu.VMEM((2, CHANS), F32),
            pltpu.VMEM((2, 2, CHANS), F32),
            pltpu.SMEM((cams,), jnp.int32),
            pltpu.VMEM((1, CHANS), F32),
            pltpu.VMEM((1, CHANS), F32),
        ]
        + [pltpu.VMEM((CHANS, CHANS), BF16)] * 4
        + [
            pltpu.VMEM((cams, CHANS), F32),
            pltpu.VMEM((2, CHANS), BF16),
            dma((15,)),
            dma((2,)),
            dma((2,)),
            dma((2,)),
            dma((tms,)),
            dma((tms // 2,)),
            dma((6,)),
            dma((6,)),
            dma((2,)),
            dma((2,)),
            dma((2,)),
            dma((2,)),
        ],
        compiler_params=pltpu.CompilerParams(
            collective_id=0, has_side_effects=True, vmem_limit_bytes=62 * 2**20
        ),
        cost_estimate=pl.CostEstimate(
            flops=flops, bytes_accessed=9 * 2**20, transcendentals=2**20
        ),
    )(
        latents.reshape(2 * CELLS, CHANS),
        cycle_position,
        conv_first.reshape(9, 3 * CHANS, CHANS),
        conv_second.reshape(9, 3 * CHANS, CHANS),
        norm_gain.reshape(1, CHANS),
        norm_shift.reshape(1, CHANS),
        w_query,
        w_key,
        w_value,
        w_out,
        camera_table,
        side_embed,
    )
    return out.reshape(shape)


def solution(mesh):
    in_specs = (P("cam", "tm", None, None, None),) + (P(),) * 11
    out_specs = P("cam", "tm", None, None, None)
    return jax.shard_map(
        on_device, mesh=mesh, in_specs=in_specs, out_specs=out_specs, check_vma=False
    )
```

```python
import functools

import jax
import jax.numpy as jnp
from jax import lax
from jax.experimental import pallas as pl
from jax.experimental.pallas import tpu as pltpu
from jax.sharding import PartitionSpec as P

GROUPS = 32
F32 = jnp.float32
BF16 = jnp.bfloat16
MESH = pl.DeviceIdType.MESH
ROWS, COLS, CHANS = 16, 32, 256
CELLS = ROWS * COLS
TALL = CELLS + 2 * COLS
SPAN = 85.0


def dot(a, b):
    return jnp.dot(a, b, preferred_element_type=F32)


def dot_t(a, b):
    return lax.dot_general(a, b, (((1,), (1,)), ((), ())), preferred_element_type=F32)


def conv_terms(buf, w, terms):
    parts = []
    for ds in range(3):
        acc = jnp.zeros((CELLS, CHANS), F32)
        for slot, dt in terms:
            for dr in range(3):
                acc += dot(
                    buf[slot, pl.ds(dr * COLS, CELLS), :],
                    w[dt * 3 + dr, pl.ds(ds * CHANS, CHANS), :],
                )
        parts.append(acc)
    col = lax.rem(lax.broadcasted_iota(jnp.int32, (CELLS, CHANS), 0), COLS)
    left = jnp.where(col == 0, 0.0, pltpu.roll(parts[0], 1, 0))
    right = jnp.where(col == COLS - 1, 0.0, pltpu.roll(parts[2], CELLS - 1, 0))
    return parts[1] + left + right


def block_kernel(
    cams,
    tms,
    lat_ref,
    place_ref,
    w1_ref,
    w2_ref,
    gain_ref,
    shift_ref,
    wq_ref,
    wk_ref,
    wv_ref,
    wo_ref,
    table_ref,
    side_ref,
    out_ref,
    xb,
    mb,
    w1,
    w2,
    first,
    part,
    code,
    nbr,
    hid,
    query,
    own,
    mate,
    st,
    fw,
    fw_in,
    place,
    gain,
    shift,
    wq,
    wk,
    wv,
    wo,
    table,
    side,
    lsem,
    hsend,
    hrecv,
    psem,
    ssend,
    srecv,
    csend,
    crecv,
    fsend,
    frecv,
    msend,
    mrecv,
):
    cam = lax.axis_index("cam")
    tm = lax.axis_index("tm")
    cam_above = lax.rem(cam + 1, cams)
    cam_below = lax.rem(cam + cams - 1, cams)
    core = lax.rem(tm, 2)
    pair = tm + 1 - 2 * core
    after = (cam, lax.rem(tm + 1, tms))
    sides_of = (cam_above, cam_below)
    chips = tms // 2
    is_first = tm == 0
    is_last = tm == tms - 1

    def later(i):
        return (cam, lax.rem(tm + i, tms))

    def remote(src, dst, send, recv, to):
        return pltpu.make_async_remote_copy(
            src_ref=src,
            dst_ref=dst,
            send_sem=send,
            recv_sem=recv,
            device_id=to,
            device_id_type=MESH,
        )

    inner = pl.ds(COLS, CELLS)
    half = [pl.ds(f * CELLS, CELLS) for f in range(2)]
    plane = [pl.ds(3 * dt, 3) for dt in range(3)]

    moves = (
        [(lat_ref.at[half[f]], xb.at[2 + f, inner]) for f in (1, 0)]
        + [(w1_ref.at[plane[dt]], w1.at[plane[dt]]) for dt in (2, 1, 0)]
        + [
            (place_ref, place),
            (table_ref, table),
            (side_ref, side),
            (gain_ref, gain),
            (shift_ref, shift),
            (wq_ref, wq),
            (wk_ref, wk),
            (wv_ref, wv),
            (wo_ref, wo),
            (w2_ref, w2),
        ]
    )
    loads = [pltpu.make_async_copy(src, dst, lsem.at[i]) for i, (src, dst) in enumerate(moves)]
    for copy in loads[:5]:
        copy.start()

    barrier = pltpu.get_barrier_semaphore()

    def greet(to):
        pl.semaphore_signal(barrier, inc=1, device_id=to, device_id_type=MESH)

    halo = [
        remote(lat_ref.at[half[f]], xb.at[f, inner], hsend.at[f], hrecv.at[f], after)
        for f in range(2)
    ]

    @pl.when(core == 0)
    def _():
        greet(later(tms - 1))
        greet((cam, pair))
        for c in sides_of:
            greet((c, tm))
            greet((c, pair))
        for i in range(1, chips):
            greet(later(2 * i))
        pl.semaphore_wait(barrier, tms + 1)

    @pl.when(core == 1)
    def _():
        greet((cam, pair))
        for c in sides_of:
            greet((c, tm))
        pl.semaphore_wait(barrier, 6)

    @pl.when(jnp.logical_not(is_last))
    def _():
        halo[1].start()
        halo[0].start()

    @pl.when(core == 1)
    def _():
        for i in range(1, chips):
            greet(later(2 * i + tms - 1))

    for copy in loads[5:]:
        copy.start()
    zero = jnp.zeros((COLS, CHANS), BF16)
    for slot in range(4):
        for at in (0, COLS + CELLS):
            xb[slot, pl.ds(at, COLS), :] = zero
            mb[slot, pl.ds(at, COLS), :] = zero
    for copy in loads[:3]:
        copy.wait()
    first[half[0], :] = conv_terms(xb, w1, [(2, 2)])
    loads[3].wait()
    first[half[1], :] = conv_terms(xb, w1, [(3, 2), (2, 1)])
    loads[4].wait()

    @pl.when(is_first)
    def _():
        xb[0, inner, :] = xb[2, inner, :]
        xb[1, inner, :] = xb[2, inner, :]

    @pl.when(jnp.logical_not(is_first))
    def _():
        halo[1].wait_recv()

    first[half[1], :] += conv_terms(xb, w1, [(1, 0)])
    first[half[0], :] += conv_terms(xb, w1, [(1, 1)])

    means, squares = [None, None], [None, None]

    def measure(f):
        rows = first[half[f], :]
        means[f] = jnp.sum(rows, axis=0, keepdims=True) / CELLS
        dev = rows - means[f]
        squares[f] = jnp.sum(dev * dev, axis=0, keepdims=True)

    measure(1)

    @pl.when(jnp.logical_not(is_first))
    def _():
        halo[0].wait_recv()

    first[half[0], :] += conv_terms(xb, w1, [(0, 0)])
    measure(0)

    def joined(mean_a, mean_b, square_a, square_b, count):
        gap = mean_b - mean_a
        return 0.5 * (mean_a + mean_b), square_a + square_b + (0.5 * count) * (gap * gap)

    mean_here, square_here = joined(means[0], means[1], squares[0], squares[1], CELLS)
    hand = remote(own, mate, psem.at[0], psem.at[1], (cam, pair))
    own[0:1, :] = mean_here
    own[1:2, :] = square_here
    swaps = [remote(st.at[0], st.at[0], ssend.at[0], srecv.at[0], (cam, pair))]
    for i in range(1, chips):
        swaps.append(remote(st.at[0], st.at[i], ssend.at[2 * i], srecv.at[i], later(2 * i)))
    for i in range(1, chips):
        swaps.append(remote(st.at[0], st.at[i], ssend.at[2 * i + 1], srecv.at[i], later(2 * i + 1)))
    far_first = sorted(range(1, chips), key=lambda i: abs(2 * i - chips))

    @pl.when(core == 0)
    def _():
        hand.wait_recv()
        mean_chip, square_chip = joined(
            mean_here, mate[0:1, :], square_here, mate[1:2, :], 2 * CELLS
        )
        st[0, 0:1, :] = mean_chip
        st[0, 1:2, :] = square_chip
        for i in far_first:
            swaps[i].start()
            swaps[i + chips - 1].start()
        swaps[0].start()

    @pl.when(core == 1)
    def _():
        hand.start()

    cam_copies = [None, None]
    for f in (1, 0):
        rows = first[half[f], :]
        code[f, pl.ds(CELLS, 16), :] = jnp.broadcast_to(means[f], (16, CHANS)).astype(BF16)
        high = code[f, pl.ds(CELLS, 16), :].astype(F32)[0:1]
        code[f, pl.ds(CELLS + 16, 16), :] = jnp.broadcast_to(means[f] - high, (16, CHANS)).astype(
            BF16
        )
        rows = rows - (high + code[f, pl.ds(CELLS + 16, 16), :].astype(F32)[0:1])
        reach = jnp.max(jnp.abs(rows), axis=0, keepdims=True)
        step = jnp.maximum(reach * (1.01 / SPAN), 1e-30)
        code[f, pl.ds(CELLS + 32, 16), :] = jnp.broadcast_to(step, (16, CHANS)).astype(BF16)
        step = code[f, pl.ds(CELLS + 32, 16), :].astype(F32)[0:1]
        code[f, pl.ds(0, CELLS), :] = jnp.exp(rows * (1.0 / step)).astype(BF16)
        cam_copies[f] = [
            remote(
                code.at[f], nbr.at[n, f], csend.at[2 * f + n], crecv.at[2 * f + n], (sides_of[n], tm)
            )
            for n in range(2)
        ]
        for copy in cam_copies[f]:
            copy.start()

    lane = lax.broadcasted_iota(jnp.int32, (8, CHANS), 1)

    def group_sum(row):
        wide = jnp.broadcast_to(row, (8, CHANS))
        for bit in (1, 2, 4):
            wide += jnp.where(
                lane & bit == 0, pltpu.roll(wide, CHANS - bit, 1), pltpu.roll(wide, bit, 1)
            )
        return wide[0:1]

    for copy in loads[5:]:
        copy.wait()
    ids = lax.broadcasted_iota(jnp.int32, (cams, CHANS), 0)
    my_place = place[cam]
    below_place = place[cam_below]
    below_is_left = below_place == lax.rem(my_place + cams - 1, cams)
    table_row = jnp.sum(jnp.where(ids == my_place, table[...], 0.0), axis=0, keepdims=True)
    extra = jnp.dot(
        jnp.broadcast_to(table_row, (8, CHANS)),
        wq[...].astype(F32),
        precision=lax.Precision.HIGHEST,
        preferred_element_type=F32,
    )[0:1]
    sides = side[...].astype(F32)
    side_below = jnp.where(below_is_left, sides[0:1], sides[1:2])
    side_above = jnp.where(below_is_left, sides[1:2], sides[0:1])
    side_wide = jnp.concatenate(
        [
            jnp.broadcast_to(side_below, (128, CHANS)),
            jnp.broadcast_to(side_above, (128, CHANS)),
        ],
        axis=0,
    ).astype(BF16)

    @pl.when(core == 1)
    def _():
        swaps[0].wait_recv()

    for copy in swaps[1:chips]:
        copy.wait_recv()
    cells = 4 * CELLS
    every = st[:, 0, :]
    mean_chan = jnp.sum(every, axis=0, keepdims=True) / chips
    away = every - mean_chan
    m2_chan = jnp.sum(st[:, 1, :], axis=0, keepdims=True) + cells * jnp.sum(
        away * away, axis=0, keepdims=True
    )
    per_group = CHANS // GROUPS
    mean = group_sum(mean_chan) / per_group
    away = mean_chan - mean
    spread = group_sum(m2_chan + (cells * chips) * (away * away)) / (
        per_group * cells * chips
    )
    scale = lax.rsqrt(spread + 1e-05) * gain[...]
    fw[0:1, :] = mean
    fw[1:2, :] = scale
    forwards = [
        remote(fw, fw_in.at[n], fsend.at[2 * n + i], frecv.at[n], (sides_of[n], t))
        for n in range(2)
        for i, t in enumerate((tm, pair))
    ]

    @pl.when(core == 1)
    def _():
        for copy in forwards:
            copy.start()

    def silu(v):
        return (v / (1.0 + jnp.exp(-v))).astype(BF16)

    for f in (1, 0):
        hid[half[f], :] = silu((first[half[f], :] - mean) * scale + shift[...])
    for f in (1, 0):
        query[half[f], :] = (dot(hid[half[f], :], wq[...]) + extra).astype(BF16)

    mixed_halo = [
        remote(mb.at[2 + f, inner], mb.at[f, inner], msend.at[f], mrecv.at[f], after)
        for f in range(2)
    ]

    for n in range(2):
        forwards[2 * n].wait_recv()

    for f in (1, 0):
        q = query[half[f], :]
        tilt = dot_t(q, side_wide)
        bias = [tilt[:, 0:1], tilt[:, 128:129]]
        scores, values = [], []

        for n in range(2):
            cam_copies[f][n].wait_recv()
            tag = nbr[n, f, pl.ds(CELLS, 48), :].astype(F32)
            scale_there = fw_in[n, 1:2, :]
            factor = tag[32:33] * scale_there
            offset = ((tag[0:1] + tag[16:17]) - fw_in[n, 0:1, :]) * scale_there + shift[...]
            rows = silu(jnp.log(nbr[n, f, pl.ds(0, CELLS), :].astype(F32)) * factor + offset)
            keys = dot(rows, wk[...]).astype(BF16)
            values.append(dot(rows, wv[...]).astype(BF16))
            scores.append((dot_t(q, keys) + bias[n]) * CHANS ** (-0.5))
        top = jnp.maximum(
            jnp.max(scores[0], axis=1, keepdims=True), jnp.max(scores[1], axis=1, keepdims=True)
        )
        expo = [jnp.exp(s - top) for s in scores]
        total = jnp.sum(expo[0], axis=1, keepdims=True) + jnp.sum(expo[1], axis=1, keepdims=True)
        inverse = 1.0 / total
        attended = (
            dot((expo[0] * inverse).astype(BF16), values[0])
            + dot((expo[1] * inverse).astype(BF16), values[1])
        ).astype(BF16)
        mixed = hid[half[f], :].astype(F32) + dot(attended, wo[...])
        mb[2 + f, inner, :] = mixed.astype(BF16)

        @pl.when(jnp.logical_not(is_last))
        def _():
            mixed_halo[f].start()

    part[half[0], :] = conv_terms(mb, w2, [(2, 2)])
    part[half[1], :] = conv_terms(mb, w2, [(3, 2), (2, 1)])

    @pl.when(is_first)
    def _():
        mb[0, inner, :] = mb[2, inner, :]
        mb[1, inner, :] = mb[2, inner, :]

    @pl.when(jnp.logical_not(is_first))
    def _():
        mixed_halo[1].wait_recv()

    total = part[half[1], :] + conv_terms(mb, w2, [(1, 0)])
    out_ref[half[1], :] = (xb[3, inner, :].astype(F32) + total).astype(BF16)
    part[half[0], :] += conv_terms(mb, w2, [(1, 1)])

    @pl.when(jnp.logical_not(is_first))
    def _():
        mixed_halo[0].wait_recv()

    total = part[half[0], :] + conv_terms(mb, w2, [(0, 0)])
    out_ref[half[0], :] = (xb[2, inner, :].astype(F32) + total).astype(BF16)

    for f in range(2):
        for copy in cam_copies[f]:
            copy.wait_send()

    @pl.when(core == 0)
    def _():
        for copy in swaps:
            copy.wait_send()

    @pl.when(core == 1)
    def _():
        hand.wait_send()
        for copy in forwards:
            copy.wait_send()

    @pl.when(jnp.logical_not(is_last))
    def _():
        for f in range(2):
            halo[f].wait_send()
            mixed_halo[f].wait_send()


def on_device(
    latents,
    cycle_position,
    conv_first,
    conv_second,
    norm_gain,
    norm_shift,
    w_query,
    w_key,
    w_value,
    w_out,
    camera_table,
    side_embed,
):
    cams, tms = lax.axis_size("cam"), lax.axis_size("tm")
    shape = latents.shape
    vmem = pl.BlockSpec(memory_space=pltpu.VMEM)
    hbm = pl.BlockSpec(memory_space=pltpu.HBM)
    dma = pltpu.SemaphoreType.DMA
    flops = 2 * 1024 * 256 * 256 * (54 + 6) + 4 * 1024 * 1024 * 256
    out = pl.pallas_call(
        functools.partial(block_kernel, cams, tms),
        out_shape=jax.ShapeDtypeStruct((2 * CELLS, CHANS), BF16),
        in_specs=[hbm] * 12,
        out_specs=vmem,
        scratch_shapes=[
            pltpu.VMEM((4, TALL, CHANS), BF16),
            pltpu.VMEM((4, TALL, CHANS), BF16),
            pltpu.VMEM((9, 3 * CHANS, CHANS), BF16),
            pltpu.VMEM((9, 3 * CHANS, CHANS), BF16),
            pltpu.VMEM((2 * CELLS, CHANS), F32),
            pltpu.VMEM((2 * CELLS, CHANS), F32),
            pltpu.VMEM((2, CELLS + 48, CHANS), BF16),
            pltpu.VMEM((2, 2, CELLS + 48, CHANS), BF16),
            pltpu.VMEM((2 * CELLS, CHANS), BF16),
            pltpu.VMEM((2 * CELLS, CHANS), BF16),
            pltpu.VMEM((2, CHANS), F32),
            pltpu.VMEM((2, CHANS), F32),
            pltpu.VMEM((tms // 2, 2, CHANS), F32),
            pltpu.VMEM((2, CHANS), F32),
            pltpu.VMEM((2, 2, CHANS), F32),
            pltpu.SMEM((cams,), jnp.int32),
            pltpu.VMEM((1, CHANS), F32),
            pltpu.VMEM((1, CHANS), F32),
        ]
        + [pltpu.VMEM((CHANS, CHANS), BF16)] * 4
        + [
            pltpu.VMEM((cams, CHANS), F32),
            pltpu.VMEM((2, CHANS), BF16),
            dma((15,)),
            dma((2,)),
            dma((2,)),
            dma((2,)),
            dma((tms,)),
            dma((tms // 2,)),
            dma((4,)),
            dma((4,)),
            dma((4,)),
            dma((2,)),
            dma((2,)),
            dma((2,)),
        ],
        compiler_params=pltpu.CompilerParams(
            collective_id=0, has_side_effects=True, vmem_limit_bytes=62 * 2**20
        ),
        cost_estimate=pl.CostEstimate(
            flops=flops, bytes_accessed=9 * 2**20, transcendentals=2**20
        ),
    )(
        latents.reshape(2 * CELLS, CHANS),
        cycle_position,
        conv_first.reshape(9, 3 * CHANS, CHANS),
        conv_second.reshape(9, 3 * CHANS, CHANS),
        norm_gain.reshape(1, CHANS),
        norm_shift.reshape(1, CHANS),
        w_query,
        w_key,
        w_value,
        w_out,
        camera_table,
        side_embed,
    )
    return out.reshape(shape)


def solution(mesh):
    in_specs = (P("cam", "tm", None, None, None),) + (P(),) * 11
    out_specs = P("cam", "tm", None, None, None)
    return jax.shard_map(
        on_device, mesh=mesh, in_specs=in_specs, out_specs=out_specs, check_vma=False
    )
```

```python
import functools

import jax
import jax.numpy as jnp
from jax import lax
from jax.experimental import pallas as pl
from jax.experimental.pallas import tpu as pltpu
from jax.sharding import PartitionSpec as P

GROUPS = 32
F32 = jnp.float32
BF16 = jnp.bfloat16
MESH = pl.DeviceIdType.MESH
ROWS, COLS, CHANS = 16, 32, 256
CELLS = ROWS * COLS
TALL = CELLS + 2 * COLS
SPAN = 85.0
CUT = 256
TILE = 256
SCORE = 1.4426950408889634 / 16.0


def dot(a, b):
    return jnp.dot(a, b, preferred_element_type=F32)


def dot_t(a, b):
    return lax.dot_general(a, b, (((1,), (1,)), ((), ())), preferred_element_type=F32)


def conv_terms(buf, w, terms):
    parts = []
    for ds in range(3):
        acc = jnp.zeros((CELLS, CHANS), F32)
        for slot, dt in terms:
            for dr in range(3):
                acc += dot(
                    buf[slot, pl.ds(dr * COLS, CELLS), :],
                    w[dt * 3 + dr, pl.ds(ds * CHANS, CHANS), :],
                )
        parts.append(acc)
    col = lax.rem(lax.broadcasted_iota(jnp.int32, (CELLS, CHANS), 0), COLS)
    left = jnp.where(col == 0, 0.0, pltpu.roll(parts[0], 1, 0))
    right = jnp.where(col == COLS - 1, 0.0, pltpu.roll(parts[2], CELLS - 1, 0))
    return parts[1] + left + right


def block_kernel(
    cams,
    tms,
    lat_ref,
    place_ref,
    w1_ref,
    w2_ref,
    gain_ref,
    shift_ref,
    wq_ref,
    wk_ref,
    wv_ref,
    wo_ref,
    table_ref,
    side_ref,
    out_ref,
    xb,
    mb,
    w1,
    w2,
    first,
    part,
    code,
    nbr,
    hid,
    query,
    own,
    mate,
    st,
    fw,
    fw_in,
    place,
    gain,
    shift,
    wq,
    wk,
    wv,
    wo,
    table,
    side,
    lsem,
    hsend,
    hrecv,
    psem,
    ssend,
    srecv,
    csend,
    crecv,
    fsend,
    frecv,
    msend,
    mrecv,
):
    cam = lax.axis_index("cam")
    tm = lax.axis_index("tm")
    cam_above = lax.rem(cam + 1, cams)
    cam_below = lax.rem(cam + cams - 1, cams)
    core = lax.rem(tm, 2)
    pair = tm + 1 - 2 * core
    after = (cam, lax.rem(tm + 1, tms))
    sides_of = (cam_above, cam_below)
    chips = tms // 2
    is_first = tm == 0
    is_last = tm == tms - 1

    def later(i):
        return (cam, lax.rem(tm + i, tms))

    def remote(src, dst, send, recv, to):
        return pltpu.make_async_remote_copy(
            src_ref=src,
            dst_ref=dst,
            send_sem=send,
            recv_sem=recv,
            device_id=to,
            device_id_type=MESH,
        )

    inner = pl.ds(COLS, CELLS)
    half = [pl.ds(f * CELLS, CELLS) for f in range(2)]
    plane = [pl.ds(3 * dt, 3) for dt in range(3)]

    moves = (
        [(lat_ref.at[half[f]], xb.at[2 + f, inner]) for f in (1, 0)]
        + [(w1_ref.at[plane[dt]], w1.at[plane[dt]]) for dt in (2, 1, 0)]
        + [
            (place_ref, place),
            (table_ref, table),
            (side_ref, side),
            (gain_ref, gain),
            (shift_ref, shift),
            (wq_ref, wq),
            (wk_ref, wk),
            (wv_ref, wv),
            (wo_ref, wo),
            (w2_ref, w2),
        ]
    )
    loads = [pltpu.make_async_copy(src, dst, lsem.at[i]) for i, (src, dst) in enumerate(moves)]
    for copy in loads[:5]:
        copy.start()

    barrier = pltpu.get_barrier_semaphore()
    far_first = sorted(range(1, chips), key=lambda i: abs(2 * i - chips))

    def greet(to):
        pl.semaphore_signal(barrier, inc=1, device_id=to, device_id_type=MESH)

    halo = [
        remote(lat_ref.at[half[f]], xb.at[f, inner], hsend.at[f], hrecv.at[f], after)
        for f in range(2)
    ]

    @pl.when(core == 0)
    def _():
        greet(later(tms - 1))
        greet((cam, pair))
        for c in sides_of:
            greet((c, tm))
            greet((c, pair))
        for i in far_first:
            greet(later(2 * i))
        pl.semaphore_wait(barrier, tms + 1)

    @pl.when(core == 1)
    def _():
        greet((cam, pair))
        for c in sides_of:
            greet((c, tm))
        for i in far_first:
            greet(later(2 * i + tms - 1))
        pl.semaphore_wait(barrier, 6)

    @pl.when(jnp.logical_not(is_last))
    def _():
        halo[1].start()
        halo[0].start()

    for copy in loads[5:14]:
        copy.start()
    zero = jnp.zeros((COLS, CHANS), BF16)
    for slot in range(4):
        for at in (0, COLS + CELLS):
            xb[slot, pl.ds(at, COLS), :] = zero
            mb[slot, pl.ds(at, COLS), :] = zero
    for copy in loads[:3]:
        copy.wait()
    first[half[0], :] = conv_terms(xb, w1, [(2, 2)])
    loads[3].wait()
    first[half[1], :] = conv_terms(xb, w1, [(3, 2), (2, 1)])
    loads[4].wait()

    @pl.when(is_first)
    def _():
        xb[0, inner, :] = xb[2, inner, :]
        xb[1, inner, :] = xb[2, inner, :]

    @pl.when(jnp.logical_not(is_first))
    def _():
        halo[1].wait_recv()

    first[half[1], :] += conv_terms(xb, w1, [(1, 0)])
    first[half[0], :] += conv_terms(xb, w1, [(1, 1)])

    means, squares = [None, None], [None, None]

    def measure(f):
        rows = first[half[f], :]
        means[f] = jnp.sum(rows, axis=0, keepdims=True) / CELLS
        dev = rows - means[f]
        squares[f] = jnp.sum(dev * dev, axis=0, keepdims=True)

    def encode(f):
        rows = first[half[f], :]
        code[f, pl.ds(CELLS, 16), :] = jnp.broadcast_to(means[f], (16, CHANS)).astype(BF16)
        high = code[f, pl.ds(CELLS, 16), :].astype(F32)[0:1]
        code[f, pl.ds(CELLS + 16, 16), :] = jnp.broadcast_to(means[f] - high, (16, CHANS)).astype(
            BF16
        )
        rows = rows - (high + code[f, pl.ds(CELLS + 16, 16), :].astype(F32)[0:1])
        reach = jnp.max(jnp.abs(rows), axis=0, keepdims=True)
        step = jnp.maximum(reach * (1.01 / SPAN), 1e-30)
        code[f, pl.ds(CELLS + 32, 16), :] = jnp.broadcast_to(step, (16, CHANS)).astype(BF16)
        step = code[f, pl.ds(CELLS + 32, 16), :].astype(F32)[0:1]
        code[f, pl.ds(0, CELLS), :] = jnp.exp(rows * (1.0 / step)).astype(BF16)

    pieces = [(1, pl.ds(0, CUT)), (1, pl.ds(CUT, CELLS + 48 - CUT)), (0, pl.ds(0, CELLS + 48))]
    cam_copies = [
        [
            remote(
                code.at[f, rows],
                nbr.at[n, f, rows],
                csend.at[2 * i + n],
                crecv.at[2 * i + n],
                (sides_of[n], tm),
            )
            for n in range(2)
        ]
        for i, (f, rows) in enumerate(pieces)
    ]

    def send_code(i):
        for copy in cam_copies[i]:
            copy.start()

    measure(1)


    @pl.when(jnp.logical_not(is_first))
    def _():
        halo[0].wait_recv()

    first[half[0], :] += conv_terms(xb, w1, [(0, 0)])
    measure(0)

    def joined(mean_a, mean_b, square_a, square_b, count):
        gap = mean_b - mean_a
        return 0.5 * (mean_a + mean_b), square_a + square_b + (0.5 * count) * (gap * gap)

    mean_here, square_here = joined(means[0], means[1], squares[0], squares[1], CELLS)
    hand = remote(own, mate, psem.at[0], psem.at[1], (cam, pair))
    own[0:1, :] = mean_here
    own[1:2, :] = square_here
    swaps = [remote(st.at[0], st.at[0], ssend.at[0], srecv.at[0], (cam, pair))]
    for i in range(1, chips):
        swaps.append(remote(st.at[0], st.at[i], ssend.at[2 * i], srecv.at[i], later(2 * i)))
    for i in range(1, chips):
        swaps.append(remote(st.at[0], st.at[i], ssend.at[2 * i + 1], srecv.at[i], later(2 * i + 1)))

    @pl.when(core == 0)
    def _():
        hand.wait_recv()
        mean_chip, square_chip = joined(
            mean_here, mate[0:1, :], square_here, mate[1:2, :], 2 * CELLS
        )
        st[0, 0:1, :] = mean_chip
        st[0, 1:2, :] = square_chip
        for i in far_first:
            swaps[i].start()
            swaps[i + chips - 1].start()
        swaps[0].start()

    @pl.when(core == 1)
    def _():
        hand.start()

    encode(1)
    send_code(0)
    send_code(1)
    encode(0)
    send_code(2)

    lane = lax.broadcasted_iota(jnp.int32, (8, CHANS), 1)

    def group_sum(row):
        wide = jnp.broadcast_to(row, (8, CHANS))
        for bit in (1, 2, 4):
            wide += jnp.where(
                lane & bit == 0, pltpu.roll(wide, CHANS - bit, 1), pltpu.roll(wide, bit, 1)
            )
        return wide[0:1]

    loads[14].start()
    for copy in loads[5:14]:
        copy.wait()
    ids = lax.broadcasted_iota(jnp.int32, (cams, CHANS), 0)
    my_place = place[cam]
    below_place = place[cam_below]
    below_is_left = below_place == lax.rem(my_place + cams - 1, cams)
    table_row = jnp.sum(jnp.where(ids == my_place, table[...], 0.0), axis=0, keepdims=True)
    extra = jnp.dot(
        jnp.broadcast_to(table_row, (8, CHANS)),
        wq[...].astype(F32),
        precision=lax.Precision.HIGHEST,
        preferred_element_type=F32,
    )[0:1]
    sides = side[...].astype(F32)
    side_below = jnp.where(below_is_left, sides[0:1], sides[1:2])
    side_above = jnp.where(below_is_left, sides[1:2], sides[0:1])
    side_wide = jnp.concatenate(
        [
            jnp.broadcast_to(side_below, (128, CHANS)),
            jnp.broadcast_to(side_above, (128, CHANS)),
        ],
        axis=0,
    ).astype(BF16)

    @pl.when(core == 1)
    def _():
        swaps[0].wait_recv()

    for copy in swaps[1:chips]:
        copy.wait_recv()
    cells = 4 * CELLS
    every = st[:, 0, :]
    mean_chan = jnp.sum(every, axis=0, keepdims=True) / chips
    away = every - mean_chan
    m2_chan = jnp.sum(st[:, 1, :], axis=0, keepdims=True) + cells * jnp.sum(
        away * away, axis=0, keepdims=True
    )
    per_group = CHANS // GROUPS
    mean = group_sum(mean_chan) / per_group
    away = mean_chan - mean
    spread = group_sum(m2_chan + (cells * chips) * (away * away)) / (
        per_group * cells * chips
    )
    scale = lax.rsqrt(spread + 1e-05) * gain[...]
    fw[0:1, :] = mean
    fw[1:2, :] = scale
    forwards = [
        remote(fw, fw_in.at[n], fsend.at[2 * n + i], frecv.at[n], (sides_of[n], t))
        for n in range(2)
        for i, t in enumerate((tm, pair))
    ]

    @pl.when(core == 1)
    def _():
        for copy in forwards:
            copy.start()

    def silu(v):
        h = 0.5 * v
        return (h + h * jnp.tanh(h)).astype(BF16)

    for f in (1, 0):
        hid[half[f], :] = silu((first[half[f], :] - mean) * scale + shift[...])
    for f in (1, 0):
        query[half[f], :] = (dot(hid[half[f], :], wq[...]) + extra).astype(BF16)

    mixed_halo = [
        [
            remote(
                mb.at[2 + f, pl.ds(COLS + i * TILE, TILE)],
                mb.at[f, pl.ds(COLS + i * TILE, TILE)],
                msend.at[2 * f + i],
                mrecv.at[2 * f + i],
                after,
            )
            for i in range(2)
        ]
        for f in range(2)
    ]
    for n in range(2):
        forwards[2 * n].wait_recv()

    for f in (1, 0):
        q = query[half[f], :]
        tilt = dot_t(q, side_wide)
        keys, values = [], []
        for n in range(2):
            for i in (0, 1) if f == 1 else (2,):
                cam_copies[i][n].wait_recv()
            tag = nbr[n, f, pl.ds(CELLS, 48), :].astype(F32)
            scale_there = fw_in[n, 1:2, :]
            factor = tag[32:33] * scale_there
            offset = ((tag[0:1] + tag[16:17]) - fw_in[n, 0:1, :]) * scale_there + shift[...]
            rows = silu(jnp.log(nbr[n, f, pl.ds(0, CELLS), :].astype(F32)) * factor + offset)
            keys.append(dot(rows, wk[...]).astype(BF16))
            values.append(dot(rows, wv[...]).astype(BF16))
        for i in range(2):
            part_rows = slice(i * TILE, (i + 1) * TILE)
            bias = [tilt[part_rows, 0:1], tilt[part_rows, 128:129]]
            raw = [dot_t(q[part_rows], keys[n]) for n in range(2)]
            tops = [jnp.max(raw[n], axis=1, keepdims=True) + bias[n] for n in range(2)]
            top = jnp.maximum(tops[0], tops[1])
            expo = [jnp.exp2(raw[n] * SCORE - (top - bias[n]) * SCORE) for n in range(2)]
            total = jnp.sum(expo[0], axis=1, keepdims=True) + jnp.sum(
                expo[1], axis=1, keepdims=True
            )
            inverse = 1.0 / total
            attended = (
                dot((expo[0] * inverse).astype(BF16), values[0])
                + dot((expo[1] * inverse).astype(BF16), values[1])
            ).astype(BF16)
            rows = pl.ds(f * CELLS + i * TILE, TILE)
            mixed = hid[rows, :].astype(F32) + dot(attended, wo[...])
            mb[2 + f, pl.ds(COLS + i * TILE, TILE), :] = mixed.astype(BF16)

            @pl.when(jnp.logical_not(is_last))
            def _():
                mixed_halo[f][i].start()

    loads[14].wait()
    part[half[0], :] = conv_terms(mb, w2, [(2, 2)])
    part[half[1], :] = conv_terms(mb, w2, [(3, 2), (2, 1)])

    @pl.when(is_first)
    def _():
        mb[0, inner, :] = mb[2, inner, :]
        mb[1, inner, :] = mb[2, inner, :]

    @pl.when(jnp.logical_not(is_first))
    def _():
        for copy in mixed_halo[1]:
            copy.wait_recv()

    total = part[half[1], :] + conv_terms(mb, w2, [(1, 0)])
    out_ref[half[1], :] = (xb[3, inner, :].astype(F32) + total).astype(BF16)
    part[half[0], :] += conv_terms(mb, w2, [(1, 1)])

    @pl.when(jnp.logical_not(is_first))
    def _():
        for copy in mixed_halo[0]:
            copy.wait_recv()

    total = part[half[0], :] + conv_terms(mb, w2, [(0, 0)])
    out_ref[half[0], :] = (xb[2, inner, :].astype(F32) + total).astype(BF16)

    for i in range(3):
        for copy in cam_copies[i]:
            copy.wait_send()

    @pl.when(core == 0)
    def _():
        for copy in swaps:
            copy.wait_send()

    @pl.when(core == 1)
    def _():
        hand.wait_send()
        for copy in forwards:
            copy.wait_send()

    @pl.when(jnp.logical_not(is_last))
    def _():
        for f in range(2):
            halo[f].wait_send()
            for copy in mixed_halo[f]:
                copy.wait_send()


def on_device(
    latents,
    cycle_position,
    conv_first,
    conv_second,
    norm_gain,
    norm_shift,
    w_query,
    w_key,
    w_value,
    w_out,
    camera_table,
    side_embed,
):
    cams, tms = lax.axis_size("cam"), lax.axis_size("tm")
    shape = latents.shape
    vmem = pl.BlockSpec(memory_space=pltpu.VMEM)
    hbm = pl.BlockSpec(memory_space=pltpu.HBM)
    dma = pltpu.SemaphoreType.DMA
    flops = 2 * 1024 * 256 * 256 * (54 + 6) + 4 * 1024 * 1024 * 256
    out = pl.pallas_call(
        functools.partial(block_kernel, cams, tms),
        out_shape=jax.ShapeDtypeStruct((2 * CELLS, CHANS), BF16),
        in_specs=[hbm] * 12,
        out_specs=vmem,
        scratch_shapes=[
            pltpu.VMEM((4, TALL, CHANS), BF16),
            pltpu.VMEM((4, TALL, CHANS), BF16),
            pltpu.VMEM((9, 3 * CHANS, CHANS), BF16),
            pltpu.VMEM((9, 3 * CHANS, CHANS), BF16),
            pltpu.VMEM((2 * CELLS, CHANS), F32),
            pltpu.VMEM((2 * CELLS, CHANS), F32),
            pltpu.VMEM((2, CELLS + 48, CHANS), BF16),
            pltpu.VMEM((2, 2, CELLS + 48, CHANS), BF16),
            pltpu.VMEM((2 * CELLS, CHANS), BF16),
            pltpu.VMEM((2 * CELLS, CHANS), BF16),
            pltpu.VMEM((2, CHANS), F32),
            pltpu.VMEM((2, CHANS), F32),
            pltpu.VMEM((tms // 2, 2, CHANS), F32),
            pltpu.VMEM((2, CHANS), F32),
            pltpu.VMEM((2, 2, CHANS), F32),
            pltpu.SMEM((cams,), jnp.int32),
            pltpu.VMEM((1, CHANS), F32),
            pltpu.VMEM((1, CHANS), F32),
        ]
        + [pltpu.VMEM((CHANS, CHANS), BF16)] * 4
        + [
            pltpu.VMEM((cams, CHANS), F32),
            pltpu.VMEM((2, CHANS), BF16),
            dma((15,)),
            dma((2,)),
            dma((2,)),
            dma((2,)),
            dma((tms,)),
            dma((tms // 2,)),
            dma((6,)),
            dma((6,)),
            dma((4,)),
            dma((2,)),
            dma((4,)),
            dma((4,)),
        ],
        compiler_params=pltpu.CompilerParams(
            collective_id=0, has_side_effects=True, vmem_limit_bytes=62 * 2**20
        ),
        cost_estimate=pl.CostEstimate(
            flops=flops, bytes_accessed=9 * 2**20, transcendentals=2**20
        ),
    )(
        latents.reshape(2 * CELLS, CHANS),
        cycle_position,
        conv_first.reshape(9, 3 * CHANS, CHANS),
        conv_second.reshape(9, 3 * CHANS, CHANS),
        norm_gain.reshape(1, CHANS),
        norm_shift.reshape(1, CHANS),
        w_query,
        w_key,
        w_value,
        w_out,
        camera_table,
        side_embed,
    )
    return out.reshape(shape)


def solution(mesh):
    in_specs = (P("cam", "tm", None, None, None),) + (P(),) * 11
    out_specs = P("cam", "tm", None, None, None)
    return jax.shard_map(
        on_device, mesh=mesh, in_specs=in_specs, out_specs=out_specs, check_vma=False
    )
```

```python
import functools

import jax
import jax.numpy as jnp
from jax import lax
from jax.experimental import pallas as pl
from jax.experimental.pallas import tpu as pltpu
from jax.sharding import PartitionSpec as P

GROUPS = 32
F32 = jnp.float32
BF16 = jnp.bfloat16
MESH = pl.DeviceIdType.MESH
ROWS, COLS, CHANS = 16, 32, 256
CELLS = ROWS * COLS
TALL = CELLS + 2 * COLS
SPAN = 85.0
CUT = 256
TILE = 256
SCORE = 1.4426950408889634 / 16.0


def dot(a, b):
    return jnp.dot(a, b, preferred_element_type=F32)


def dot_t(a, b):
    return lax.dot_general(a, b, (((1,), (1,)), ((), ())), preferred_element_type=F32)


def conv_terms(buf, w, terms):
    parts = []
    for ds in range(3):
        acc = jnp.zeros((CELLS, CHANS), F32)
        for slot, dt in terms:
            for dr in range(3):
                acc += dot(
                    buf[slot, pl.ds(dr * COLS, CELLS), :],
                    w[dt * 3 + dr, pl.ds(ds * CHANS, CHANS), :],
                )
        parts.append(acc)
    col = lax.rem(lax.broadcasted_iota(jnp.int32, (CELLS, CHANS), 0), COLS)
    left = jnp.where(col == 0, 0.0, pltpu.roll(parts[0], 1, 0))
    right = jnp.where(col == COLS - 1, 0.0, pltpu.roll(parts[2], CELLS - 1, 0))
    return parts[1] + left + right


def block_kernel(
    cams,
    tms,
    lat_ref,
    place_ref,
    w1_ref,
    w2_ref,
    gain_ref,
    shift_ref,
    wq_ref,
    wk_ref,
    wv_ref,
    wo_ref,
    table_ref,
    side_ref,
    out_ref,
    xb,
    mb,
    w1,
    w2,
    first,
    part,
    code,
    nbr,
    hid,
    query,
    own,
    mate,
    st,
    fw,
    fw_in,
    place,
    gain,
    shift,
    wq,
    wk,
    wv,
    wo,
    table,
    side,
    lsem,
    hsend,
    hrecv,
    psem,
    ssend,
    srecv,
    csend,
    crecv,
    fsend,
    frecv,
    msend,
    mrecv,
):
    cam = lax.axis_index("cam")
    tm = lax.axis_index("tm")
    cam_above = lax.rem(cam + 1, cams)
    cam_below = lax.rem(cam + cams - 1, cams)
    core = lax.rem(tm, 2)
    pair = tm + 1 - 2 * core
    after = (cam, lax.rem(tm + 1, tms))
    sides_of = (cam_above, cam_below)
    chips = tms // 2
    is_first = tm == 0
    is_last = tm == tms - 1

    def later(i):
        return (cam, lax.rem(tm + i, tms))

    def remote(src, dst, send, recv, to):
        return pltpu.make_async_remote_copy(
            src_ref=src,
            dst_ref=dst,
            send_sem=send,
            recv_sem=recv,
            device_id=to,
            device_id_type=MESH,
        )

    inner = pl.ds(COLS, CELLS)
    half = [pl.ds(f * CELLS, CELLS) for f in range(2)]
    plane = [pl.ds(3 * dt, 3) for dt in range(3)]

    moves = (
        [(lat_ref.at[half[f]], xb.at[2 + f, inner]) for f in (1, 0)]
        + [(w1_ref.at[plane[dt]], w1.at[plane[dt]]) for dt in (2, 1, 0)]
        + [
            (place_ref, place),
            (table_ref, table),
            (side_ref, side),
            (gain_ref, gain),
            (shift_ref, shift),
            (wq_ref, wq),
            (wk_ref, wk),
            (wv_ref, wv),
            (wo_ref, wo),
            (w2_ref, w2),
        ]
    )
    loads = [pltpu.make_async_copy(src, dst, lsem.at[i]) for i, (src, dst) in enumerate(moves)]
    for copy in loads[:5]:
        copy.start()

    barrier = pltpu.get_barrier_semaphore()
    far_first = sorted(range(1, chips), key=lambda i: abs(2 * i - chips))

    def greet(to):
        pl.semaphore_signal(barrier, inc=1, device_id=to, device_id_type=MESH)

    halo = [
        remote(xb.at[2 + f, inner], xb.at[f, inner], hsend.at[f], hrecv.at[f], after)
        for f in range(2)
    ]

    @pl.when(core == 0)
    def _():
        greet(later(tms - 1))
        greet((cam, pair))
        for c in sides_of:
            greet((c, tm))
            greet((c, pair))
        for i in far_first:
            greet(later(2 * i))
        pl.semaphore_wait(barrier, tms + 1)

    @pl.when(core == 1)
    def _():
        greet((cam, pair))
        for c in sides_of:
            greet((c, tm))
        for i in far_first:
            greet(later(2 * i + tms - 1))
        pl.semaphore_wait(barrier, 6)

    for copy in loads[:2]:
        copy.wait()

    @pl.when(jnp.logical_not(is_last))
    def _():
        halo[1].start()
        halo[0].start()

    for copy in loads[5:14]:
        copy.start()
    zero = jnp.zeros((COLS, CHANS), BF16)
    for slot in range(4):
        for at in (0, COLS + CELLS):
            xb[slot, pl.ds(at, COLS), :] = zero
            mb[slot, pl.ds(at, COLS), :] = zero
    loads[2].wait()
    first[half[0], :] = conv_terms(xb, w1, [(2, 2)])
    loads[3].wait()
    first[half[1], :] = conv_terms(xb, w1, [(3, 2), (2, 1)])
    loads[4].wait()

    @pl.when(is_first)
    def _():
        xb[0, inner, :] = xb[2, inner, :]
        xb[1, inner, :] = xb[2, inner, :]

    @pl.when(jnp.logical_not(is_first))
    def _():
        halo[1].wait_recv()

    first[half[1], :] += conv_terms(xb, w1, [(1, 0)])
    first[half[0], :] += conv_terms(xb, w1, [(1, 1)])

    means, squares = [None, None], [None, None]

    def measure(f):
        rows = first[half[f], :]
        means[f] = jnp.sum(rows, axis=0, keepdims=True) / CELLS
        dev = rows - means[f]
        squares[f] = jnp.sum(dev * dev, axis=0, keepdims=True)

    def encode(f):
        rows = first[half[f], :]
        marks = pl.ds(CELLS, 16)
        code[f, marks, :] = jnp.broadcast_to(means[f], (16, CHANS)).astype(BF16)
        low = means[f] - code[f, marks, :].astype(F32)[0:1]
        line = lax.broadcasted_iota(jnp.int32, (16, CHANS), 0)
        code[f, marks, :] = jnp.where(line < 8, means[f], low).astype(BF16)
        tag = code[f, marks, :].astype(F32)
        rows = rows - (tag[0:1] + tag[8:9])
        reach = jnp.max(jnp.abs(rows), axis=0, keepdims=True)
        step = jnp.maximum(reach * (1.01 / SPAN), 1e-30)
        code[f, marks, :] = jnp.where(line < 12, tag, step).astype(BF16)
        step = code[f, marks, :].astype(F32)[12:13]
        code[f, pl.ds(0, CELLS), :] = jnp.exp(rows * (1.0 / step)).astype(BF16)

    pieces = [(1, pl.ds(0, CUT)), (1, pl.ds(CUT, CELLS + 16 - CUT)), (0, pl.ds(0, CELLS + 16))]
    cam_copies = [
        [
            remote(
                code.at[f, rows],
                nbr.at[n, f, rows],
                csend.at[2 * i + n],
                crecv.at[2 * i + n],
                (sides_of[n], tm),
            )
            for n in range(2)
        ]
        for i, (f, rows) in enumerate(pieces)
    ]

    def send_code(i):
        for copy in cam_copies[i]:
            copy.start()

    measure(1)


    @pl.when(jnp.logical_not(is_first))
    def _():
        halo[0].wait_recv()

    first[half[0], :] += conv_terms(xb, w1, [(0, 0)])
    measure(0)

    def joined(mean_a, mean_b, square_a, square_b, count):
        gap = mean_b - mean_a
        return 0.5 * (mean_a + mean_b), square_a + square_b + (0.5 * count) * (gap * gap)

    mean_here, square_here = joined(means[0], means[1], squares[0], squares[1], CELLS)
    hand = remote(own, mate, psem.at[0], psem.at[1], (cam, pair))
    own[0:1, :] = mean_here
    own[1:2, :] = square_here
    swaps = [remote(st.at[0], st.at[0], ssend.at[0], srecv.at[0], (cam, pair))]
    for i in range(1, chips):
        swaps.append(remote(st.at[0], st.at[i], ssend.at[2 * i], srecv.at[i], later(2 * i)))
    for i in range(1, chips):
        swaps.append(remote(st.at[0], st.at[i], ssend.at[2 * i + 1], srecv.at[i], later(2 * i + 1)))

    @pl.when(core == 0)
    def _():
        hand.wait_recv()
        mean_chip, square_chip = joined(
            mean_here, mate[0:1, :], square_here, mate[1:2, :], 2 * CELLS
        )
        st[0, 0:1, :] = mean_chip
        st[0, 1:2, :] = square_chip
        for i in far_first:
            swaps[i].start()
            swaps[i + chips - 1].start()
        swaps[0].start()

    @pl.when(core == 1)
    def _():
        hand.start()

    encode(1)
    send_code(0)
    send_code(1)
    encode(0)
    send_code(2)

    lane = lax.broadcasted_iota(jnp.int32, (8, CHANS), 1)

    def group_sum(row):
        wide = jnp.broadcast_to(row, (8, CHANS))
        for bit in (1, 2, 4):
            wide += jnp.where(
                lane & bit == 0, pltpu.roll(wide, CHANS - bit, 1), pltpu.roll(wide, bit, 1)
            )
        return wide[0:1]

    loads[14].start()
    for copy in loads[5:14]:
        copy.wait()
    ids = lax.broadcasted_iota(jnp.int32, (cams, CHANS), 0)
    my_place = place[cam]
    below_place = place[cam_below]
    below_is_left = below_place == lax.rem(my_place + cams - 1, cams)
    table_row = jnp.sum(jnp.where(ids == my_place, table[...], 0.0), axis=0, keepdims=True)
    extra = jnp.dot(
        jnp.broadcast_to(table_row, (8, CHANS)),
        wq[...].astype(F32),
        precision=lax.Precision.HIGHEST,
        preferred_element_type=F32,
    )[0:1]
    sides = side[...].astype(F32)
    side_below = jnp.where(below_is_left, sides[0:1], sides[1:2])
    side_above = jnp.where(below_is_left, sides[1:2], sides[0:1])
    side_wide = jnp.concatenate(
        [
            jnp.broadcast_to(side_below, (128, CHANS)),
            jnp.broadcast_to(side_above, (128, CHANS)),
        ],
        axis=0,
    ).astype(BF16)

    @pl.when(core == 1)
    def _():
        swaps[0].wait_recv()

    for copy in swaps[1:chips]:
        copy.wait_recv()
    cells = 4 * CELLS
    every = st[:, 0, :]
    mean_chan = jnp.sum(every, axis=0, keepdims=True) / chips
    away = every - mean_chan
    m2_chan = jnp.sum(st[:, 1, :], axis=0, keepdims=True) + cells * jnp.sum(
        away * away, axis=0, keepdims=True
    )
    per_group = CHANS // GROUPS
    mean = group_sum(mean_chan) / per_group
    away = mean_chan - mean
    spread = group_sum(m2_chan + (cells * chips) * (away * away)) / (
        per_group * cells * chips
    )
    scale = lax.rsqrt(spread + 1e-05) * gain[...]
    fw[0:1, :] = mean
    fw[1:2, :] = scale
    forwards = [
        remote(fw, fw_in.at[n], fsend.at[2 * n + i], frecv.at[n], (sides_of[n], t))
        for n in range(2)
        for i, t in enumerate((tm, pair))
    ]

    @pl.when(core == 1)
    def _():
        for copy in forwards:
            copy.start()

    def silu(v):
        h = 0.5 * v
        return (h + h * jnp.tanh(h)).astype(BF16)

    for f in (1, 0):
        hid[half[f], :] = silu((first[half[f], :] - mean) * scale + shift[...])
    for f in (1, 0):
        query[half[f], :] = (dot(hid[half[f], :], wq[...]) + extra).astype(BF16)

    mixed_halo = [
        [
            remote(
                mb.at[2 + f, pl.ds(COLS + i * TILE, TILE)],
                mb.at[f, pl.ds(COLS + i * TILE, TILE)],
                msend.at[2 * f + i],
                mrecv.at[2 * f + i],
                after,
            )
            for i in range(2)
        ]
        for f in range(2)
    ]
    tilts = [dot_t(query[half[f], :], side_wide) for f in range(2)]
    for n in range(2):
        forwards[2 * n].wait_recv()

    for f in (1, 0):
        q = query[half[f], :]
        tilt = tilts[f]
        keys, values = [], []
        for n in range(2):
            for i in (0, 1) if f == 1 else (2,):
                cam_copies[i][n].wait_recv()
            tag = nbr[n, f, pl.ds(CELLS, 16), :].astype(F32)
            scale_there = fw_in[n, 1:2, :]
            factor = tag[12:13] * scale_there
            offset = ((tag[0:1] + tag[8:9]) - fw_in[n, 0:1, :]) * scale_there + shift[...]
            rows = silu(jnp.log(nbr[n, f, pl.ds(0, CELLS), :].astype(F32)) * factor + offset)
            keys.append(dot(rows, wk[...]).astype(BF16))
            values.append(dot(rows, wv[...]).astype(BF16))
        for i in range(2):
            part_rows = slice(i * TILE, (i + 1) * TILE)
            bias = [tilt[part_rows, 0:1], tilt[part_rows, 128:129]]
            raw = [dot_t(q[part_rows], keys[n]) for n in range(2)]
            tops = [jnp.max(raw[n], axis=1, keepdims=True) + bias[n] for n in range(2)]
            top = jnp.maximum(tops[0], tops[1])
            expo = [jnp.exp2(raw[n] * SCORE - (top - bias[n]) * SCORE) for n in range(2)]
            total = jnp.sum(expo[0], axis=1, keepdims=True) + jnp.sum(
                expo[1], axis=1, keepdims=True
            )
            inverse = 1.0 / total
            attended = (
                dot((expo[0] * inverse).astype(BF16), values[0])
                + dot((expo[1] * inverse).astype(BF16), values[1])
            ).astype(BF16)
            rows = pl.ds(f * CELLS + i * TILE, TILE)
            mixed = hid[rows, :].astype(F32) + dot(attended, wo[...])
            mb[2 + f, pl.ds(COLS + i * TILE, TILE), :] = mixed.astype(BF16)

            @pl.when(jnp.logical_not(is_last))
            def _():
                mixed_halo[f][i].start()

    loads[14].wait()
    part[half[0], :] = conv_terms(mb, w2, [(2, 2)])
    part[half[1], :] = conv_terms(mb, w2, [(3, 2), (2, 1)])

    @pl.when(is_first)
    def _():
        mb[0, inner, :] = mb[2, inner, :]
        mb[1, inner, :] = mb[2, inner, :]

    @pl.when(jnp.logical_not(is_first))
    def _():
        for copy in mixed_halo[1]:
            copy.wait_recv()

    total = part[half[1], :] + conv_terms(mb, w2, [(1, 0)])
    out_ref[half[1], :] = (xb[3, inner, :].astype(F32) + total).astype(BF16)
    part[half[0], :] += conv_terms(mb, w2, [(1, 1)])

    @pl.when(jnp.logical_not(is_first))
    def _():
        for copy in mixed_halo[0]:
            copy.wait_recv()

    total = part[half[0], :] + conv_terms(mb, w2, [(0, 0)])
    out_ref[half[0], :] = (xb[2, inner, :].astype(F32) + total).astype(BF16)

    for i in range(3):
        for copy in cam_copies[i]:
            copy.wait_send()

    @pl.when(core == 0)
    def _():
        for copy in swaps:
            copy.wait_send()

    @pl.when(core == 1)
    def _():
        hand.wait_send()
        for copy in forwards:
            copy.wait_send()

    @pl.when(jnp.logical_not(is_last))
    def _():
        for f in range(2):
            halo[f].wait_send()
            for copy in mixed_halo[f]:
                copy.wait_send()


def on_device(
    latents,
    cycle_position,
    conv_first,
    conv_second,
    norm_gain,
    norm_shift,
    w_query,
    w_key,
    w_value,
    w_out,
    camera_table,
    side_embed,
):
    cams, tms = lax.axis_size("cam"), lax.axis_size("tm")
    shape = latents.shape
    vmem = pl.BlockSpec(memory_space=pltpu.VMEM)
    hbm = pl.BlockSpec(memory_space=pltpu.HBM)
    dma = pltpu.SemaphoreType.DMA
    flops = 2 * 1024 * 256 * 256 * (54 + 6) + 4 * 1024 * 1024 * 256
    out = pl.pallas_call(
        functools.partial(block_kernel, cams, tms),
        out_shape=jax.ShapeDtypeStruct((2 * CELLS, CHANS), BF16),
        in_specs=[hbm] * 12,
        out_specs=vmem,
        scratch_shapes=[
            pltpu.VMEM((4, TALL, CHANS), BF16),
            pltpu.VMEM((4, TALL, CHANS), BF16),
            pltpu.VMEM((9, 3 * CHANS, CHANS), BF16),
            pltpu.VMEM((9, 3 * CHANS, CHANS), BF16),
            pltpu.VMEM((2 * CELLS, CHANS), F32),
            pltpu.VMEM((2 * CELLS, CHANS), F32),
            pltpu.VMEM((2, CELLS + 16, CHANS), BF16),
            pltpu.VMEM((2, 2, CELLS + 16, CHANS), BF16),
            pltpu.VMEM((2 * CELLS, CHANS), BF16),
            pltpu.VMEM((2 * CELLS, CHANS), BF16),
            pltpu.VMEM((2, CHANS), F32),
            pltpu.VMEM((2, CHANS), F32),
            pltpu.VMEM((tms // 2, 2, CHANS), F32),
            pltpu.VMEM((2, CHANS), F32),
            pltpu.VMEM((2, 2, CHANS), F32),
            pltpu.SMEM((cams,), jnp.int32),
            pltpu.VMEM((1, CHANS), F32),
            pltpu.VMEM((1, CHANS), F32),
        ]
        + [pltpu.VMEM((CHANS, CHANS), BF16)] * 4
        + [
            pltpu.VMEM((cams, CHANS), F32),
            pltpu.VMEM((2, CHANS), BF16),
            dma((15,)),
            dma((2,)),
            dma((2,)),
            dma((2,)),
            dma((tms,)),
            dma((tms // 2,)),
            dma((6,)),
            dma((6,)),
            dma((4,)),
            dma((2,)),
            dma((4,)),
            dma((4,)),
        ],
        compiler_params=pltpu.CompilerParams(
            collective_id=0, has_side_effects=True, vmem_limit_bytes=62 * 2**20
        ),
        cost_estimate=pl.CostEstimate(
            flops=flops, bytes_accessed=9 * 2**20, transcendentals=2**20
        ),
    )(
        latents.reshape(2 * CELLS, CHANS),
        cycle_position,
        conv_first.reshape(9, 3 * CHANS, CHANS),
        conv_second.reshape(9, 3 * CHANS, CHANS),
        norm_gain.reshape(1, CHANS),
        norm_shift.reshape(1, CHANS),
        w_query,
        w_key,
        w_value,
        w_out,
        camera_table,
        side_embed,
    )
    return out.reshape(shape)


def solution(mesh):
    in_specs = (P("cam", "tm", None, None, None),) + (P(),) * 11
    out_specs = P("cam", "tm", None, None, None)
    return jax.shard_map(
        on_device, mesh=mesh, in_specs=in_specs, out_specs=out_specs, check_vma=False
    )
```

```python
import functools

import jax
import jax.numpy as jnp
from jax import lax
from jax.experimental import pallas as pl
from jax.experimental.pallas import tpu as pltpu
from jax.sharding import PartitionSpec as P

GROUPS = 32
F32 = jnp.float32
BF16 = jnp.bfloat16
MESH = pl.DeviceIdType.MESH
ROWS, COLS, CHANS = 16, 32, 256
CELLS = ROWS * COLS
TALL = CELLS + 2 * COLS
SPAN = 85.0
CUT = 256
TILE = 256
SCORE = 1.4426950408889634 / 16.0


def dot(a, b):
    return jnp.dot(a, b, preferred_element_type=F32)


def dot_t(a, b):
    return lax.dot_general(a, b, (((1,), (1,)), ((), ())), preferred_element_type=F32)


def conv_terms(buf, w, terms):
    parts = []
    for ds in range(3):
        acc = jnp.zeros((CELLS, CHANS), F32)
        for slot, dt in terms:
            for dr in range(3):
                acc += dot(
                    buf[slot, pl.ds(dr * COLS, CELLS), :],
                    w[dt * 3 + dr, pl.ds(ds * CHANS, CHANS), :],
                )
        parts.append(acc)
    col = lax.rem(lax.broadcasted_iota(jnp.int32, (CELLS, CHANS), 0), COLS)
    left = jnp.where(col == 0, 0.0, pltpu.roll(parts[0], 1, 0))
    right = jnp.where(col == COLS - 1, 0.0, pltpu.roll(parts[2], CELLS - 1, 0))
    return parts[1] + left + right


def block_kernel(
    cams,
    tms,
    lat_ref,
    place_ref,
    w1_ref,
    w2_ref,
    gain_ref,
    shift_ref,
    wq_ref,
    wk_ref,
    wv_ref,
    wo_ref,
    table_ref,
    side_ref,
    out_ref,
    xb,
    mb,
    w1,
    w2,
    first,
    part,
    code,
    nbr,
    hid,
    query,
    own,
    mate,
    st,
    fw,
    fw_in,
    place,
    gain,
    shift,
    wq,
    wk,
    wv,
    wo,
    table,
    side,
    lsem,
    hsend,
    hrecv,
    psem,
    ssend,
    srecv,
    csend,
    crecv,
    fsend,
    frecv,
    msend,
    mrecv,
):
    cam = lax.axis_index("cam")
    tm = lax.axis_index("tm")
    cam_above = lax.rem(cam + 1, cams)
    cam_below = lax.rem(cam + cams - 1, cams)
    core = lax.rem(tm, 2)
    pair = tm + 1 - 2 * core
    after = (cam, lax.rem(tm + 1, tms))
    sides_of = (cam_above, cam_below)
    chips = tms // 2
    is_first = tm == 0
    is_last = tm == tms - 1

    def later(i):
        return (cam, lax.rem(tm + i, tms))

    def remote(src, dst, send, recv, to):
        return pltpu.make_async_remote_copy(
            src_ref=src,
            dst_ref=dst,
            send_sem=send,
            recv_sem=recv,
            device_id=to,
            device_id_type=MESH,
        )

    inner = pl.ds(COLS, CELLS)
    half = [pl.ds(f * CELLS, CELLS) for f in range(2)]
    plane = [pl.ds(3 * dt, 3) for dt in range(3)]

    moves = (
        [(lat_ref.at[half[f]], xb.at[2 + f, inner]) for f in (1, 0)]
        + [(w1_ref.at[plane[dt]], w1.at[plane[dt]]) for dt in (2, 1, 0)]
        + [
            (place_ref, place),
            (table_ref, table),
            (side_ref, side),
            (gain_ref, gain),
            (shift_ref, shift),
            (wq_ref, wq),
            (wk_ref, wk),
            (wv_ref, wv),
            (wo_ref, wo),
            (w2_ref, w2),
        ]
    )
    loads = [pltpu.make_async_copy(src, dst, lsem.at[i]) for i, (src, dst) in enumerate(moves)]
    for copy in loads[:5]:
        copy.start()

    barrier = pltpu.get_barrier_semaphore()
    far_first = sorted(range(1, chips), key=lambda i: abs(2 * i - chips))

    def greet(to):
        pl.semaphore_signal(barrier, inc=1, device_id=to, device_id_type=MESH)

    halo = [
        remote(xb.at[2 + f, inner], xb.at[f, inner], hsend.at[f], hrecv.at[f], after)
        for f in range(2)
    ]

    @pl.when(core == 0)
    def _():
        greet(later(tms - 1))
        greet((cam, pair))
        for c in sides_of:
            greet((c, tm))
            greet((c, pair))
        for i in far_first:
            greet(later(2 * i))
        pl.semaphore_wait(barrier, tms + 1)

    @pl.when(core == 1)
    def _():
        greet((cam, pair))
        for c in sides_of:
            greet((c, tm))
        for i in far_first:
            greet(later(2 * i + tms - 1))
        pl.semaphore_wait(barrier, 6)

    for copy in loads[:2]:
        copy.wait()

    @pl.when(jnp.logical_not(is_last))
    def _():
        halo[1].start()
        halo[0].start()

    for copy in loads[5:14]:
        copy.start()
    zero = jnp.zeros((COLS, CHANS), BF16)
    for slot in range(4):
        for at in (0, COLS + CELLS):
            xb[slot, pl.ds(at, COLS), :] = zero
            mb[slot, pl.ds(at, COLS), :] = zero
    loads[2].wait()
    first[half[0], :] = conv_terms(xb, w1, [(2, 2)])
    loads[3].wait()
    first[half[1], :] = conv_terms(xb, w1, [(3, 2), (2, 1)])
    loads[4].wait()

    @pl.when(is_first)
    def _():
        xb[0, inner, :] = xb[2, inner, :]
        xb[1, inner, :] = xb[2, inner, :]

    @pl.when(jnp.logical_not(is_first))
    def _():
        halo[1].wait_recv()

    first[half[1], :] += conv_terms(xb, w1, [(1, 0)])
    first[half[0], :] += conv_terms(xb, w1, [(1, 1)])

    means, squares = [None, None], [None, None]

    def measure(f):
        rows = first[half[f], :]
        means[f] = jnp.sum(rows, axis=0, keepdims=True) / CELLS
        dev = rows - means[f]
        squares[f] = jnp.sum(dev * dev, axis=0, keepdims=True)

    def encode(f):
        rows = first[half[f], :]
        marks = pl.ds(CELLS, 16)
        code[f, marks, :] = jnp.broadcast_to(means[f], (16, CHANS)).astype(BF16)
        low = means[f] - code[f, marks, :].astype(F32)[0:1]
        line = lax.broadcasted_iota(jnp.int32, (16, CHANS), 0)
        code[f, marks, :] = jnp.where(line < 8, means[f], low).astype(BF16)
        tag = code[f, marks, :].astype(F32)
        rows = rows - (tag[0:1] + tag[8:9])
        reach = jnp.max(jnp.abs(rows), axis=0, keepdims=True)
        step = jnp.maximum(reach * (1.01 / SPAN), 1e-30)
        code[f, marks, :] = jnp.where(line < 12, tag, step).astype(BF16)
        step = code[f, marks, :].astype(F32)[12:13]
        code[f, pl.ds(0, CELLS), :] = jnp.exp(rows * (1.0 / step)).astype(BF16)

    pieces = [(1, pl.ds(0, CUT)), (1, pl.ds(CUT, CELLS + 16 - CUT)), (0, pl.ds(0, CELLS + 16))]
    cam_copies = [
        [
            remote(
                code.at[f, rows],
                nbr.at[n, f, rows],
                csend.at[2 * i + n],
                crecv.at[2 * i + n],
                (sides_of[n], tm),
            )
            for n in range(2)
        ]
        for i, (f, rows) in enumerate(pieces)
    ]

    def send_code(i):
        for copy in cam_copies[i]:
            copy.start()

    measure(1)


    @pl.when(jnp.logical_not(is_first))
    def _():
        halo[0].wait_recv()

    first[half[0], :] += conv_terms(xb, w1, [(0, 0)])
    measure(0)

    def joined(mean_a, mean_b, square_a, square_b, count):
        gap = mean_b - mean_a
        return 0.5 * (mean_a + mean_b), square_a + square_b + (0.5 * count) * (gap * gap)

    mean_here, square_here = joined(means[0], means[1], squares[0], squares[1], CELLS)
    hand = remote(own, mate, psem.at[0], psem.at[1], (cam, pair))
    own[0:1, :] = mean_here
    own[1:2, :] = square_here
    swaps = [remote(st.at[0], st.at[0], ssend.at[0], srecv.at[0], (cam, pair))]
    for i in range(1, chips):
        swaps.append(remote(st.at[0], st.at[i], ssend.at[2 * i], srecv.at[i], later(2 * i)))
    for i in range(1, chips):
        swaps.append(remote(st.at[0], st.at[i], ssend.at[2 * i + 1], srecv.at[i], later(2 * i + 1)))

    @pl.when(core == 0)
    def _():
        hand.wait_recv()
        mean_chip, square_chip = joined(
            mean_here, mate[0:1, :], square_here, mate[1:2, :], 2 * CELLS
        )
        st[0, 0:1, :] = mean_chip
        st[0, 1:2, :] = square_chip
        for i in far_first:
            swaps[i + chips - 1].start()
        swaps[0].start()
        for i in far_first:
            swaps[i].start()

    @pl.when(core == 1)
    def _():
        hand.start()

    encode(1)
    send_code(0)
    send_code(1)
    encode(0)
    send_code(2)

    lane = lax.broadcasted_iota(jnp.int32, (8, CHANS), 1)

    def group_sum(row):
        wide = jnp.broadcast_to(row, (8, CHANS))
        for bit in (1, 2, 4):
            wide += jnp.where(
                lane & bit == 0, pltpu.roll(wide, CHANS - bit, 1), pltpu.roll(wide, bit, 1)
            )
        return wide[0:1]

    loads[14].start()
    for copy in loads[5:14]:
        copy.wait()
    ids = lax.broadcasted_iota(jnp.int32, (cams, CHANS), 0)
    my_place = place[cam]
    below_place = place[cam_below]
    below_is_left = below_place == lax.rem(my_place + cams - 1, cams)
    table_row = jnp.sum(jnp.where(ids == my_place, table[...], 0.0), axis=0, keepdims=True)
    extra = jnp.dot(
        jnp.broadcast_to(table_row, (8, CHANS)),
        wq[...].astype(F32),
        precision=lax.Precision.HIGHEST,
        preferred_element_type=F32,
    )[0:1]
    sides = side[...].astype(F32)
    side_below = jnp.where(below_is_left, sides[0:1], sides[1:2])
    side_above = jnp.where(below_is_left, sides[1:2], sides[0:1])
    side_wide = jnp.concatenate(
        [
            jnp.broadcast_to(side_below, (128, CHANS)),
            jnp.broadcast_to(side_above, (128, CHANS)),
        ],
        axis=0,
    ).astype(BF16)

    @pl.when(core == 1)
    def _():
        swaps[0].wait_recv()

    for copy in swaps[1:chips]:
        copy.wait_recv()
    cells = 4 * CELLS
    every = st[:, 0, :]
    mean_chan = jnp.sum(every, axis=0, keepdims=True) / chips
    away = every - mean_chan
    m2_chan = jnp.sum(st[:, 1, :], axis=0, keepdims=True) + cells * jnp.sum(
        away * away, axis=0, keepdims=True
    )
    per_group = CHANS // GROUPS
    mean = group_sum(mean_chan) / per_group
    away = mean_chan - mean
    spread = group_sum(m2_chan + (cells * chips) * (away * away)) / (
        per_group * cells * chips
    )
    scale = lax.rsqrt(spread + 1e-05) * gain[...]
    fw[0:1, :] = mean
    fw[1:2, :] = scale
    forwards = [
        remote(fw, fw_in.at[n], fsend.at[2 * n + i], frecv.at[n], (sides_of[n], t))
        for n in range(2)
        for i, t in enumerate((tm, pair))
    ]

    @pl.when(core == 1)
    def _():
        for copy in forwards:
            copy.start()

    def silu(v):
        h = 0.5 * v
        return (h + h * jnp.tanh(h)).astype(BF16)

    for f in (1, 0):
        hid[half[f], :] = silu((first[half[f], :] - mean) * scale + shift[...])
    for f in (1, 0):
        query[half[f], :] = (dot(hid[half[f], :], wq[...]) + extra).astype(BF16)

    mixed_halo = [
        [
            remote(
                mb.at[2 + f, pl.ds(COLS + i * TILE, TILE)],
                mb.at[f, pl.ds(COLS + i * TILE, TILE)],
                msend.at[2 * f + i],
                mrecv.at[2 * f + i],
                after,
            )
            for i in range(2)
        ]
        for f in range(2)
    ]
    tilts = [dot_t(query[half[f], :], side_wide) for f in range(2)]
    for n in range(2):
        forwards[2 * n].wait_recv()

    for f in (1, 0):
        q = query[half[f], :]
        tilt = tilts[f]
        there = []
        for n in range(2):
            for i in (0, 1) if f == 1 else (2,):
                cam_copies[i][n].wait_recv()
            tag = nbr[n, f, pl.ds(CELLS, 16), :].astype(F32)
            scale_there = fw_in[n, 1:2, :]
            factor = tag[12:13] * scale_there
            offset = ((tag[0:1] + tag[8:9]) - fw_in[n, 0:1, :]) * scale_there + shift[...]
            there.append(silu(jnp.log(nbr[n, f, pl.ds(0, CELLS), :].astype(F32)) * factor + offset))
        keys = [dot(rows, wk[...]).astype(BF16) for rows in there]
        values = [dot(rows, wv[...]).astype(BF16) for rows in there]
        attended = []
        for i in range(2):
            part_rows = slice(i * TILE, (i + 1) * TILE)
            bias = [tilt[part_rows, 0:1], tilt[part_rows, 128:129]]
            raw = [dot_t(q[part_rows], keys[n]) for n in range(2)]
            tops = [jnp.max(raw[n], axis=1, keepdims=True) + bias[n] for n in range(2)]
            top = jnp.maximum(tops[0], tops[1])
            expo = [jnp.exp2(raw[n] * SCORE - (top - bias[n]) * SCORE) for n in range(2)]
            total = jnp.sum(expo[0], axis=1, keepdims=True) + jnp.sum(
                expo[1], axis=1, keepdims=True
            )
            inverse = 1.0 / total
            attended.append(
                (
                    dot((expo[0] * inverse).astype(BF16), values[0])
                    + dot((expo[1] * inverse).astype(BF16), values[1])
                ).astype(BF16)
            )
        for i in range(2):
            rows = pl.ds(f * CELLS + i * TILE, TILE)
            mixed = hid[rows, :].astype(F32) + dot(attended[i], wo[...])
            mb[2 + f, pl.ds(COLS + i * TILE, TILE), :] = mixed.astype(BF16)

        @pl.when(jnp.logical_not(is_last))
        def _():
            for copy in mixed_halo[f]:
                copy.start()

    loads[14].wait()
    part[half[0], :] = conv_terms(mb, w2, [(2, 2)])
    part[half[1], :] = conv_terms(mb, w2, [(3, 2), (2, 1)])

    @pl.when(is_first)
    def _():
        mb[0, inner, :] = mb[2, inner, :]
        mb[1, inner, :] = mb[2, inner, :]

    @pl.when(jnp.logical_not(is_first))
    def _():
        for copy in mixed_halo[1]:
            copy.wait_recv()

    total = part[half[1], :] + conv_terms(mb, w2, [(1, 0)])
    out_ref[half[1], :] = (xb[3, inner, :].astype(F32) + total).astype(BF16)
    part[half[0], :] += conv_terms(mb, w2, [(1, 1)])

    @pl.when(jnp.logical_not(is_first))
    def _():
        for copy in mixed_halo[0]:
            copy.wait_recv()

    total = part[half[0], :] + conv_terms(mb, w2, [(0, 0)])
    out_ref[half[0], :] = (xb[2, inner, :].astype(F32) + total).astype(BF16)

    for i in range(3):
        for copy in cam_copies[i]:
            copy.wait_send()

    @pl.when(core == 0)
    def _():
        for copy in swaps:
            copy.wait_send()

    @pl.when(core == 1)
    def _():
        hand.wait_send()
        for copy in forwards:
            copy.wait_send()

    @pl.when(jnp.logical_not(is_last))
    def _():
        for f in range(2):
            halo[f].wait_send()
            for copy in mixed_halo[f]:
                copy.wait_send()


def on_device(
    latents,
    cycle_position,
    conv_first,
    conv_second,
    norm_gain,
    norm_shift,
    w_query,
    w_key,
    w_value,
    w_out,
    camera_table,
    side_embed,
):
    cams, tms = lax.axis_size("cam"), lax.axis_size("tm")
    shape = latents.shape
    vmem = pl.BlockSpec(memory_space=pltpu.VMEM)
    hbm = pl.BlockSpec(memory_space=pltpu.HBM)
    dma = pltpu.SemaphoreType.DMA
    flops = 2 * 1024 * 256 * 256 * (54 + 6) + 4 * 1024 * 1024 * 256
    out = pl.pallas_call(
        functools.partial(block_kernel, cams, tms),
        out_shape=jax.ShapeDtypeStruct((2 * CELLS, CHANS), BF16),
        in_specs=[hbm] * 12,
        out_specs=vmem,
        scratch_shapes=[
            pltpu.VMEM((4, TALL, CHANS), BF16),
            pltpu.VMEM((4, TALL, CHANS), BF16),
            pltpu.VMEM((9, 3 * CHANS, CHANS), BF16),
            pltpu.VMEM((9, 3 * CHANS, CHANS), BF16),
            pltpu.VMEM((2 * CELLS, CHANS), F32),
            pltpu.VMEM((2 * CELLS, CHANS), F32),
            pltpu.VMEM((2, CELLS + 16, CHANS), BF16),
            pltpu.VMEM((2, 2, CELLS + 16, CHANS), BF16),
            pltpu.VMEM((2 * CELLS, CHANS), BF16),
            pltpu.VMEM((2 * CELLS, CHANS), BF16),
            pltpu.VMEM((2, CHANS), F32),
            pltpu.VMEM((2, CHANS), F32),
            pltpu.VMEM((tms // 2, 2, CHANS), F32),
            pltpu.VMEM((2, CHANS), F32),
            pltpu.VMEM((2, 2, CHANS), F32),
            pltpu.SMEM((cams,), jnp.int32),
            pltpu.VMEM((1, CHANS), F32),
            pltpu.VMEM((1, CHANS), F32),
        ]
        + [pltpu.VMEM((CHANS, CHANS), BF16)] * 4
        + [
            pltpu.VMEM((cams, CHANS), F32),
            pltpu.VMEM((2, CHANS), BF16),
            dma((15,)),
            dma((2,)),
            dma((2,)),
            dma((2,)),
            dma((tms,)),
            dma((tms // 2,)),
            dma((6,)),
            dma((6,)),
            dma((4,)),
            dma((2,)),
            dma((4,)),
            dma((4,)),
        ],
        compiler_params=pltpu.CompilerParams(
            collective_id=0, has_side_effects=True, vmem_limit_bytes=62 * 2**20
        ),
        cost_estimate=pl.CostEstimate(
            flops=flops, bytes_accessed=9 * 2**20, transcendentals=2**20
        ),
    )(
        latents.reshape(2 * CELLS, CHANS),
        cycle_position,
        conv_first.reshape(9, 3 * CHANS, CHANS),
        conv_second.reshape(9, 3 * CHANS, CHANS),
        norm_gain.reshape(1, CHANS),
        norm_shift.reshape(1, CHANS),
        w_query,
        w_key,
        w_value,
        w_out,
        camera_table,
        side_embed,
    )
    return out.reshape(shape)


def solution(mesh):
    in_specs = (P("cam", "tm", None, None, None),) + (P(),) * 11
    out_specs = P("cam", "tm", None, None, None)
    return jax.shard_map(
        on_device, mesh=mesh, in_specs=in_specs, out_specs=out_specs, check_vma=False
    )
```

```python
import functools

import jax
import jax.numpy as jnp
from jax import lax
from jax.experimental import pallas as pl
from jax.experimental.pallas import tpu as pltpu
from jax.sharding import PartitionSpec as P

GROUPS = 32
F32 = jnp.float32
BF16 = jnp.bfloat16
MESH = pl.DeviceIdType.MESH
ROWS, COLS, CHANS = 16, 32, 256
CELLS = ROWS * COLS
TALL = CELLS + 2 * COLS
SPAN = 85.0
CUT = 256
TILE = 256
CHUNKS = ((0, TILE + COLS), (TILE + COLS, CELLS - TILE - COLS))
SCORE = 1.4426950408889634 / 16.0


def dot(a, b):
    return jnp.dot(a, b, preferred_element_type=F32)


def dot_t(a, b):
    return lax.dot_general(a, b, (((1,), (1,)), ((), ())), preferred_element_type=F32)


def conv_terms(buf, w, terms, at=0, size=CELLS):
    parts = []
    for ds in range(3):
        acc = jnp.zeros((size, CHANS), F32)
        for slot, dt in terms:
            for dr in range(3):
                acc += dot(
                    buf[slot, pl.ds(at + dr * COLS, size), :],
                    w[dt * 3 + dr, pl.ds(ds * CHANS, CHANS), :],
                )
        parts.append(acc)
    col = lax.rem(lax.broadcasted_iota(jnp.int32, (size, CHANS), 0), COLS)
    left = jnp.where(col == 0, 0.0, pltpu.roll(parts[0], 1, 0))
    right = jnp.where(col == COLS - 1, 0.0, pltpu.roll(parts[2], size - 1, 0))
    return parts[1] + left + right


def block_kernel(
    cams,
    tms,
    lat_ref,
    place_ref,
    w1_ref,
    w2_ref,
    gain_ref,
    shift_ref,
    wq_ref,
    wk_ref,
    wv_ref,
    wo_ref,
    table_ref,
    side_ref,
    out_ref,
    xb,
    mb,
    w1,
    w2,
    first,
    part,
    code,
    nbr,
    hid,
    query,
    own,
    mate,
    st,
    fw,
    fw_in,
    place,
    gain,
    shift,
    wq,
    wk,
    wv,
    wo,
    table,
    side,
    lsem,
    hsend,
    hrecv,
    psem,
    ssend,
    srecv,
    csend,
    crecv,
    fsend,
    frecv,
    msend,
    mrecv,
):
    cam = lax.axis_index("cam")
    tm = lax.axis_index("tm")
    cam_above = lax.rem(cam + 1, cams)
    cam_below = lax.rem(cam + cams - 1, cams)
    core = lax.rem(tm, 2)
    pair = tm + 1 - 2 * core
    after = (cam, lax.rem(tm + 1, tms))
    sides_of = (cam_above, cam_below)
    chips = tms // 2
    is_first = tm == 0
    is_last = tm == tms - 1

    def later(i):
        return (cam, lax.rem(tm + i, tms))

    def remote(src, dst, send, recv, to):
        return pltpu.make_async_remote_copy(
            src_ref=src,
            dst_ref=dst,
            send_sem=send,
            recv_sem=recv,
            device_id=to,
            device_id_type=MESH,
        )

    inner = pl.ds(COLS, CELLS)
    half = [pl.ds(f * CELLS, CELLS) for f in range(2)]
    plane = [pl.ds(3 * dt, 3) for dt in range(3)]

    moves = (
        [(lat_ref.at[half[f]], xb.at[2 + f, inner]) for f in (1, 0)]
        + [(w1_ref.at[plane[dt]], w1.at[plane[dt]]) for dt in (2, 1, 0)]
        + [
            (place_ref, place),
            (table_ref, table),
            (side_ref, side),
            (gain_ref, gain),
            (shift_ref, shift),
            (wq_ref, wq),
            (wk_ref, wk),
            (wv_ref, wv),
            (wo_ref, wo),
            (w2_ref, w2),
        ]
    )
    loads = [pltpu.make_async_copy(src, dst, lsem.at[i]) for i, (src, dst) in enumerate(moves)]
    for copy in loads[:5]:
        copy.start()

    barrier = pltpu.get_barrier_semaphore()
    far_first = sorted(range(1, chips), key=lambda i: abs(2 * i - chips))

    def greet(to):
        pl.semaphore_signal(barrier, inc=1, device_id=to, device_id_type=MESH)

    halo = [
        remote(
            xb.at[2 + f, pl.ds(COLS + at, size)],
            xb.at[f, pl.ds(COLS + at, size)],
            hsend.at[i],
            hrecv.at[i],
            after,
        )
        for i, (f, at, size) in enumerate(((1, 0, CELLS),) + tuple((0,) + c for c in CHUNKS))
    ]

    @pl.when(core == 0)
    def _():
        greet(later(tms - 1))
        greet((cam, pair))
        for c in sides_of:
            greet((c, tm))
            greet((c, pair))
        for i in far_first:
            greet(later(2 * i))
        pl.semaphore_wait(barrier, tms + 1)

    @pl.when(core == 1)
    def _():
        greet((cam, pair))
        for c in sides_of:
            greet((c, tm))
        for i in far_first:
            greet(later(2 * i + tms - 1))
        pl.semaphore_wait(barrier, 6)

    for copy in loads[:2]:
        copy.wait()

    @pl.when(jnp.logical_not(is_last))
    def _():
        for copy in halo:
            copy.start()

    for copy in loads[5:14]:
        copy.start()
    zero = jnp.zeros((COLS, CHANS), BF16)
    for slot in range(4):
        for at in (0, COLS + CELLS):
            xb[slot, pl.ds(at, COLS), :] = zero
            mb[slot, pl.ds(at, COLS), :] = zero
    loads[2].wait()
    first[half[0], :] = conv_terms(xb, w1, [(2, 2)])
    loads[3].wait()
    first[half[1], :] = conv_terms(xb, w1, [(3, 2), (2, 1)])
    loads[4].wait()

    @pl.when(is_first)
    def _():
        xb[0, inner, :] = xb[2, inner, :]
        xb[1, inner, :] = xb[2, inner, :]

    @pl.when(jnp.logical_not(is_first))
    def _():
        halo[0].wait_recv()

    first[half[1], :] += conv_terms(xb, w1, [(1, 0)])
    first[half[0], :] += conv_terms(xb, w1, [(1, 1)])

    means, squares = [None, None], [None, None]

    def measure(f):
        rows = first[half[f], :]
        means[f] = jnp.sum(rows, axis=0, keepdims=True) / CELLS
        dev = rows - means[f]
        squares[f] = jnp.sum(dev * dev, axis=0, keepdims=True)

    def encode(f):
        rows = first[half[f], :]
        marks = pl.ds(CELLS, 16)
        code[f, marks, :] = jnp.broadcast_to(means[f], (16, CHANS)).astype(BF16)
        low = means[f] - code[f, marks, :].astype(F32)[0:1]
        line = lax.broadcasted_iota(jnp.int32, (16, CHANS), 0)
        code[f, marks, :] = jnp.where(line < 8, means[f], low).astype(BF16)
        tag = code[f, marks, :].astype(F32)
        rows = rows - (tag[0:1] + tag[8:9])
        reach = jnp.max(jnp.abs(rows), axis=0, keepdims=True)
        step = jnp.maximum(reach * (1.01 / SPAN), 1e-30)
        code[f, marks, :] = jnp.where(line < 12, tag, step).astype(BF16)
        step = code[f, marks, :].astype(F32)[12:13]
        code[f, pl.ds(0, CELLS), :] = jnp.exp(rows * (1.0 / step)).astype(BF16)

    pieces = [(1, pl.ds(0, CUT)), (1, pl.ds(CUT, CELLS + 16 - CUT)), (0, pl.ds(0, CELLS + 16))]
    cam_copies = [
        [
            remote(
                code.at[f, rows],
                nbr.at[n, f, rows],
                csend.at[2 * i + n],
                crecv.at[2 * i + n],
                (sides_of[n], tm),
            )
            for n in range(2)
        ]
        for i, (f, rows) in enumerate(pieces)
    ]

    def send_code(i):
        for copy in cam_copies[i]:
            copy.start()

    measure(1)


    for i in range(2):

        @pl.when(jnp.logical_not(is_first))
        def _():
            halo[1 + i].wait_recv()

        first[pl.ds(i * TILE, TILE), :] += conv_terms(xb, w1, [(0, 0)], i * TILE, TILE)
    measure(0)

    def joined(mean_a, mean_b, square_a, square_b, count):
        gap = mean_b - mean_a
        return 0.5 * (mean_a + mean_b), square_a + square_b + (0.5 * count) * (gap * gap)

    mean_here, square_here = joined(means[0], means[1], squares[0], squares[1], CELLS)
    hand = remote(own, mate, psem.at[0], psem.at[1], (cam, pair))
    own[0:1, :] = mean_here
    own[1:2, :] = square_here
    swaps = [remote(st.at[0], st.at[0], ssend.at[0], srecv.at[0], (cam, pair))]
    for i in range(1, chips):
        swaps.append(remote(st.at[0], st.at[i], ssend.at[2 * i], srecv.at[i], later(2 * i)))
    for i in range(1, chips):
        swaps.append(remote(st.at[0], st.at[i], ssend.at[2 * i + 1], srecv.at[i], later(2 * i + 1)))

    @pl.when(core == 0)
    def _():
        hand.wait_recv()
        mean_chip, square_chip = joined(
            mean_here, mate[0:1, :], square_here, mate[1:2, :], 2 * CELLS
        )
        st[0, 0:1, :] = mean_chip
        st[0, 1:2, :] = square_chip
        for i in far_first:
            swaps[i + chips - 1].start()
        swaps[0].start()
        for i in far_first:
            swaps[i].start()

    @pl.when(core == 1)
    def _():
        hand.start()

    encode(1)
    send_code(0)
    send_code(1)
    encode(0)
    send_code(2)

    lane = lax.broadcasted_iota(jnp.int32, (8, CHANS), 1)

    def group_sum(row):
        wide = jnp.broadcast_to(row, (8, CHANS))
        for bit in (1, 2, 4):
            wide += jnp.where(
                lane & bit == 0, pltpu.roll(wide, CHANS - bit, 1), pltpu.roll(wide, bit, 1)
            )
        return wide[0:1]

    loads[14].start()
    for copy in loads[5:14]:
        copy.wait()
    ids = lax.broadcasted_iota(jnp.int32, (cams, CHANS), 0)
    my_place = place[cam]
    below_place = place[cam_below]
    below_is_left = below_place == lax.rem(my_place + cams - 1, cams)
    table_row = jnp.sum(jnp.where(ids == my_place, table[...], 0.0), axis=0, keepdims=True)
    extra = jnp.dot(
        jnp.broadcast_to(table_row, (8, CHANS)),
        wq[...].astype(F32),
        precision=lax.Precision.HIGHEST,
        preferred_element_type=F32,
    )[0:1]
    sides = side[...].astype(F32)
    side_below = jnp.where(below_is_left, sides[0:1], sides[1:2])
    side_above = jnp.where(below_is_left, sides[1:2], sides[0:1])
    side_wide = jnp.concatenate(
        [
            jnp.broadcast_to(side_below, (128, CHANS)),
            jnp.broadcast_to(side_above, (128, CHANS)),
        ],
        axis=0,
    ).astype(BF16)

    @pl.when(core == 1)
    def _():
        swaps[0].wait_recv()

    for copy in swaps[1:chips]:
        copy.wait_recv()
    cells = 4 * CELLS
    every = st[:, 0, :]
    mean_chan = jnp.sum(every, axis=0, keepdims=True) / chips
    away = every - mean_chan
    m2_chan = jnp.sum(st[:, 1, :], axis=0, keepdims=True) + cells * jnp.sum(
        away * away, axis=0, keepdims=True
    )
    per_group = CHANS // GROUPS
    mean = group_sum(mean_chan) / per_group
    away = mean_chan - mean
    spread = group_sum(m2_chan + (cells * chips) * (away * away)) / (
        per_group * cells * chips
    )
    scale = lax.rsqrt(spread + 1e-05) * gain[...]
    fw[0:1, :] = mean
    fw[1:2, :] = scale
    forwards = [
        remote(fw, fw_in.at[n], fsend.at[2 * n + i], frecv.at[n], (sides_of[n], t))
        for n in range(2)
        for i, t in enumerate((tm, pair))
    ]

    @pl.when(core == 1)
    def _():
        for copy in forwards:
            copy.start()

    def silu(v):
        h = 0.5 * v
        return (h + h * jnp.tanh(h)).astype(BF16)

    for f in (1, 0):
        hid[half[f], :] = silu((first[half[f], :] - mean) * scale + shift[...])
    for f in (1, 0):
        query[half[f], :] = (dot(hid[half[f], :], wq[...]) + extra).astype(BF16)

    mixed_halo = [
        [
            remote(
                mb.at[2 + f, pl.ds(COLS + at, size)],
                mb.at[f, pl.ds(COLS + at, size)],
                msend.at[2 * f + i],
                mrecv.at[2 * f + i],
                after,
            )
            for i, (at, size) in enumerate(CHUNKS)
        ]
        for f in range(2)
    ]
    tilts = [dot_t(query[half[f], :], side_wide) for f in range(2)]
    for n in range(2):
        forwards[2 * n].wait_recv()

    for f in (1, 0):
        q = query[half[f], :]
        tilt = tilts[f]
        there = []
        for n in range(2):
            for i in (0, 1) if f == 1 else (2,):
                cam_copies[i][n].wait_recv()
            tag = nbr[n, f, pl.ds(CELLS, 16), :].astype(F32)
            scale_there = fw_in[n, 1:2, :]
            factor = tag[12:13] * scale_there
            offset = ((tag[0:1] + tag[8:9]) - fw_in[n, 0:1, :]) * scale_there + shift[...]
            there.append(silu(jnp.log(nbr[n, f, pl.ds(0, CELLS), :].astype(F32)) * factor + offset))
        keys = [dot(rows, wk[...]).astype(BF16) for rows in there]
        values = [dot(rows, wv[...]).astype(BF16) for rows in there]
        attended = []
        for i in range(2):
            part_rows = slice(i * TILE, (i + 1) * TILE)
            bias = [tilt[part_rows, 0:1], tilt[part_rows, 128:129]]
            raw = [dot_t(q[part_rows], keys[n]) for n in range(2)]
            tops = [jnp.max(raw[n], axis=1, keepdims=True) + bias[n] for n in range(2)]
            top = jnp.maximum(tops[0], tops[1])
            expo = [jnp.exp2(raw[n] * SCORE - (top - bias[n]) * SCORE) for n in range(2)]
            total = jnp.sum(expo[0], axis=1, keepdims=True) + jnp.sum(
                expo[1], axis=1, keepdims=True
            )
            inverse = 1.0 / total
            attended.append(
                (
                    dot((expo[0] * inverse).astype(BF16), values[0])
                    + dot((expo[1] * inverse).astype(BF16), values[1])
                ).astype(BF16)
            )
        for i in range(2):
            rows = pl.ds(f * CELLS + i * TILE, TILE)
            mixed = hid[rows, :].astype(F32) + dot(attended[i], wo[...])
            mb[2 + f, pl.ds(COLS + i * TILE, TILE), :] = mixed.astype(BF16)

        @pl.when(jnp.logical_not(is_last))
        def _():
            for copy in mixed_halo[f]:
                copy.start()

    loads[14].wait()
    part[half[0], :] = conv_terms(mb, w2, [(2, 2)])
    part[half[1], :] = conv_terms(mb, w2, [(3, 2), (2, 1)])

    @pl.when(is_first)
    def _():
        mb[0, inner, :] = mb[2, inner, :]
        mb[1, inner, :] = mb[2, inner, :]

    @pl.when(jnp.logical_not(is_first))
    def _():
        for copy in mixed_halo[1]:
            copy.wait_recv()

    total = part[half[1], :] + conv_terms(mb, w2, [(1, 0)])
    out_ref[half[1], :] = (xb[3, inner, :].astype(F32) + total).astype(BF16)
    part[half[0], :] += conv_terms(mb, w2, [(1, 1)])

    for i in range(2):

        @pl.when(jnp.logical_not(is_first))
        def _():
            mixed_halo[0][i].wait_recv()

        rows = pl.ds(i * TILE, TILE)
        total = part[rows, :] + conv_terms(mb, w2, [(0, 0)], i * TILE, TILE)
        out_ref[rows, :] = (xb[2, pl.ds(COLS + i * TILE, TILE), :].astype(F32) + total).astype(BF16)

    for i in range(3):
        for copy in cam_copies[i]:
            copy.wait_send()

    @pl.when(core == 0)
    def _():
        for copy in swaps:
            copy.wait_send()

    @pl.when(core == 1)
    def _():
        hand.wait_send()
        for copy in forwards:
            copy.wait_send()

    @pl.when(jnp.logical_not(is_last))
    def _():
        for copy in halo:
            copy.wait_send()
        for f in range(2):
            for copy in mixed_halo[f]:
                copy.wait_send()


def on_device(
    latents,
    cycle_position,
    conv_first,
    conv_second,
    norm_gain,
    norm_shift,
    w_query,
    w_key,
    w_value,
    w_out,
    camera_table,
    side_embed,
):
    cams, tms = lax.axis_size("cam"), lax.axis_size("tm")
    shape = latents.shape
    vmem = pl.BlockSpec(memory_space=pltpu.VMEM)
    hbm = pl.BlockSpec(memory_space=pltpu.HBM)
    dma = pltpu.SemaphoreType.DMA
    flops = 2 * 1024 * 256 * 256 * (54 + 6) + 4 * 1024 * 1024 * 256
    out = pl.pallas_call(
        functools.partial(block_kernel, cams, tms),
        out_shape=jax.ShapeDtypeStruct((2 * CELLS, CHANS), BF16),
        in_specs=[hbm] * 12,
        out_specs=vmem,
        scratch_shapes=[
            pltpu.VMEM((4, TALL, CHANS), BF16),
            pltpu.VMEM((4, TALL, CHANS), BF16),
            pltpu.VMEM((9, 3 * CHANS, CHANS), BF16),
            pltpu.VMEM((9, 3 * CHANS, CHANS), BF16),
            pltpu.VMEM((2 * CELLS, CHANS), F32),
            pltpu.VMEM((2 * CELLS, CHANS), F32),
            pltpu.VMEM((2, CELLS + 16, CHANS), BF16),
            pltpu.VMEM((2, 2, CELLS + 16, CHANS), BF16),
            pltpu.VMEM((2 * CELLS, CHANS), BF16),
            pltpu.VMEM((2 * CELLS, CHANS), BF16),
            pltpu.VMEM((2, CHANS), F32),
            pltpu.VMEM((2, CHANS), F32),
            pltpu.VMEM((tms // 2, 2, CHANS), F32),
            pltpu.VMEM((2, CHANS), F32),
            pltpu.VMEM((2, 2, CHANS), F32),
            pltpu.SMEM((cams,), jnp.int32),
            pltpu.VMEM((1, CHANS), F32),
            pltpu.VMEM((1, CHANS), F32),
        ]
        + [pltpu.VMEM((CHANS, CHANS), BF16)] * 4
        + [
            pltpu.VMEM((cams, CHANS), F32),
            pltpu.VMEM((2, CHANS), BF16),
            dma((15,)),
            dma((3,)),
            dma((3,)),
            dma((2,)),
            dma((tms,)),
            dma((tms // 2,)),
            dma((6,)),
            dma((6,)),
            dma((4,)),
            dma((2,)),
            dma((4,)),
            dma((4,)),
        ],
        compiler_params=pltpu.CompilerParams(
            collective_id=0, has_side_effects=True, vmem_limit_bytes=62 * 2**20
        ),
        cost_estimate=pl.CostEstimate(
            flops=flops, bytes_accessed=9 * 2**20, transcendentals=2**20
        ),
    )(
        latents.reshape(2 * CELLS, CHANS),
        cycle_position,
        conv_first.reshape(9, 3 * CHANS, CHANS),
        conv_second.reshape(9, 3 * CHANS, CHANS),
        norm_gain.reshape(1, CHANS),
        norm_shift.reshape(1, CHANS),
        w_query,
        w_key,
        w_value,
        w_out,
        camera_table,
        side_embed,
    )
    return out.reshape(shape)


def solution(mesh):
    in_specs = (P("cam", "tm", None, None, None),) + (P(),) * 11
    out_specs = P("cam", "tm", None, None, None)
    return jax.shard_map(
        on_device, mesh=mesh, in_specs=in_specs, out_specs=out_specs, check_vma=False
    )
```

```python
import functools

import jax
import jax.numpy as jnp
from jax import lax
from jax.experimental import pallas as pl
from jax.experimental.pallas import tpu as pltpu
from jax.sharding import PartitionSpec as P

GROUPS = 32
F32 = jnp.float32
BF16 = jnp.bfloat16
MESH = pl.DeviceIdType.MESH
ROWS, COLS, CHANS = 16, 32, 256
CELLS = ROWS * COLS
TALL = CELLS + 2 * COLS
SPAN = 85.0
CUT = 256
TILE = 256
CHUNKS = ((0, TILE + COLS), (TILE + COLS, CELLS - TILE - COLS))
SCORE = 1.4426950408889634 / 16.0


def dot(a, b):
    return jnp.dot(a, b, preferred_element_type=F32)


def dot_t(a, b):
    return lax.dot_general(a, b, (((1,), (1,)), ((), ())), preferred_element_type=F32)


def conv_terms(buf, w, terms, at=0, size=CELLS):
    parts = []
    for ds in range(3):
        acc = jnp.zeros((size, CHANS), F32)
        for slot, dt in terms:
            for dr in range(3):
                acc += dot(
                    buf[slot, pl.ds(at + dr * COLS, size), :],
                    w[dt * 3 + dr, pl.ds(ds * CHANS, CHANS), :],
                )
        parts.append(acc)
    col = lax.rem(lax.broadcasted_iota(jnp.int32, (size, CHANS), 0), COLS)
    left = jnp.where(col == 0, 0.0, pltpu.roll(parts[0], 1, 0))
    right = jnp.where(col == COLS - 1, 0.0, pltpu.roll(parts[2], size - 1, 0))
    return parts[1] + left + right


def block_kernel(
    cams,
    tms,
    lat_ref,
    place_ref,
    w1_ref,
    w2_ref,
    gain_ref,
    shift_ref,
    wq_ref,
    wk_ref,
    wv_ref,
    wo_ref,
    table_ref,
    side_ref,
    out_ref,
    xb,
    mb,
    w1,
    w2,
    first,
    part,
    code,
    nbr,
    hid,
    query,
    own,
    mate,
    st,
    fw,
    fw_in,
    place,
    gain,
    shift,
    wq,
    wk,
    wv,
    wo,
    table,
    side,
    lsem,
    hsend,
    hrecv,
    psem,
    ssend,
    srecv,
    csend,
    crecv,
    fsend,
    frecv,
    msend,
    mrecv,
):
    cam = lax.axis_index("cam")
    tm = lax.axis_index("tm")
    cam_above = lax.rem(cam + 1, cams)
    cam_below = lax.rem(cam + cams - 1, cams)
    core = lax.rem(tm, 2)
    pair = tm + 1 - 2 * core
    after = (cam, lax.rem(tm + 1, tms))
    sides_of = (cam_above, cam_below)
    chips = tms // 2
    is_first = tm == 0
    is_last = tm == tms - 1

    def later(i):
        return (cam, lax.rem(tm + i, tms))

    def remote(src, dst, send, recv, to):
        return pltpu.make_async_remote_copy(
            src_ref=src,
            dst_ref=dst,
            send_sem=send,
            recv_sem=recv,
            device_id=to,
            device_id_type=MESH,
        )

    inner = pl.ds(COLS, CELLS)
    half = [pl.ds(f * CELLS, CELLS) for f in range(2)]
    plane = [pl.ds(3 * dt, 3) for dt in range(3)]

    moves = (
        [(lat_ref.at[half[f]], xb.at[2 + f, inner]) for f in (1, 0)]
        + [(w1_ref.at[plane[dt]], w1.at[plane[dt]]) for dt in (2, 1, 0)]
        + [
            (place_ref, place),
            (table_ref, table),
            (side_ref, side),
            (gain_ref, gain),
            (shift_ref, shift),
            (wq_ref, wq),
            (wk_ref, wk),
            (wv_ref, wv),
            (wo_ref, wo),
            (w2_ref, w2),
        ]
    )
    loads = [pltpu.make_async_copy(src, dst, lsem.at[i]) for i, (src, dst) in enumerate(moves)]
    for copy in loads[:5]:
        copy.start()

    barrier = pltpu.get_barrier_semaphore()
    far_first = sorted(range(1, chips), key=lambda i: abs(2 * i - chips))

    def greet(to):
        pl.semaphore_signal(barrier, inc=1, device_id=to, device_id_type=MESH)

    halo = [
        remote(
            xb.at[2 + f, pl.ds(COLS + at, size)],
            xb.at[f, pl.ds(COLS + at, size)],
            hsend.at[i],
            hrecv.at[i],
            after,
        )
        for i, (f, at, size) in enumerate(((1, 0, CELLS),) + tuple((0,) + c for c in CHUNKS))
    ]

    @pl.when(core == 0)
    def _():
        greet(later(tms - 1))
        greet((cam, pair))
        for c in sides_of:
            greet((c, tm))
            greet((c, pair))
        for i in far_first:
            greet(later(2 * i))
        pl.semaphore_wait(barrier, tms + 1)

    @pl.when(core == 1)
    def _():
        greet((cam, pair))
        for c in sides_of:
            greet((c, tm))
        for i in far_first:
            greet(later(2 * i + tms - 1))
        pl.semaphore_wait(barrier, 6)

    for copy in loads[:2]:
        copy.wait()

    @pl.when(jnp.logical_not(is_last))
    def _():
        for copy in halo:
            copy.start()

    for copy in loads[5:14]:
        copy.start()
    zero = jnp.zeros((COLS, CHANS), BF16)
    for slot in range(4):
        for at in (0, COLS + CELLS):
            xb[slot, pl.ds(at, COLS), :] = zero
            mb[slot, pl.ds(at, COLS), :] = zero
    loads[2].wait()
    first[half[0], :] = conv_terms(xb, w1, [(2, 2)])
    loads[3].wait()
    first[half[1], :] = conv_terms(xb, w1, [(3, 2), (2, 1)])
    loads[4].wait()

    @pl.when(is_first)
    def _():
        xb[0, inner, :] = xb[2, inner, :]
        xb[1, inner, :] = xb[2, inner, :]

    @pl.when(jnp.logical_not(is_first))
    def _():
        halo[0].wait_recv()

    first[half[1], :] += conv_terms(xb, w1, [(1, 0)])
    first[half[0], :] += conv_terms(xb, w1, [(1, 1)])

    means, squares = [None, None], [None, None]

    def measure(f):
        rows = first[half[f], :]
        means[f] = jnp.sum(rows, axis=0, keepdims=True) / CELLS
        dev = rows - means[f]
        squares[f] = jnp.sum(dev * dev, axis=0, keepdims=True)

    def encode(f):
        rows = first[half[f], :]
        marks = pl.ds(CELLS, 16)
        code[f, marks, :] = jnp.broadcast_to(means[f], (16, CHANS)).astype(BF16)
        low = means[f] - code[f, marks, :].astype(F32)[0:1]
        line = lax.broadcasted_iota(jnp.int32, (16, CHANS), 0)
        code[f, marks, :] = jnp.where(line < 8, means[f], low).astype(BF16)
        tag = code[f, marks, :].astype(F32)
        rows = rows - (tag[0:1] + tag[8:9])
        reach = jnp.max(jnp.abs(rows), axis=0, keepdims=True)
        step = jnp.maximum(reach * (1.01 / SPAN), 1e-30)
        code[f, marks, :] = jnp.where(line < 12, tag, step).astype(BF16)
        step = code[f, marks, :].astype(F32)[12:13]
        code[f, pl.ds(0, CELLS), :] = jnp.exp(rows * (1.0 / step)).astype(BF16)

    pieces = [(1, pl.ds(0, CUT)), (1, pl.ds(CUT, CELLS + 16 - CUT)), (0, pl.ds(0, CELLS + 16))]
    cam_copies = [
        [
            remote(
                code.at[f, rows],
                nbr.at[n, f, rows],
                csend.at[2 * i + n],
                crecv.at[2 * i + n],
                (sides_of[n], tm),
            )
            for n in range(2)
        ]
        for i, (f, rows) in enumerate(pieces)
    ]

    def send_code(i):
        for copy in cam_copies[i]:
            copy.start()

    measure(1)


    tile_means, tile_squares = [], []
    for i in range(2):

        @pl.when(jnp.logical_not(is_first))
        def _():
            halo[1 + i].wait_recv()

        rows = pl.ds(i * TILE, TILE)
        first[rows, :] += conv_terms(xb, w1, [(0, 0)], i * TILE, TILE)
        tile_means.append(jnp.sum(first[rows, :], axis=0, keepdims=True) / TILE)
        dev = first[rows, :] - tile_means[i]
        tile_squares.append(jnp.sum(dev * dev, axis=0, keepdims=True))

    def joined(mean_a, mean_b, square_a, square_b, count):
        gap = mean_b - mean_a
        return 0.5 * (mean_a + mean_b), square_a + square_b + (0.5 * count) * (gap * gap)

    means[0], squares[0] = joined(*tile_means, *tile_squares, TILE)
    mean_here, square_here = joined(means[0], means[1], squares[0], squares[1], CELLS)
    hand = remote(own, mate, psem.at[0], psem.at[1], (cam, pair))
    own[0:1, :] = mean_here
    own[1:2, :] = square_here
    swaps = [remote(st.at[0], st.at[0], ssend.at[0], srecv.at[0], (cam, pair))]
    for i in range(1, chips):
        swaps.append(remote(st.at[0], st.at[i], ssend.at[2 * i], srecv.at[i], later(2 * i)))
    for i in range(1, chips):
        swaps.append(remote(st.at[0], st.at[i], ssend.at[2 * i + 1], srecv.at[i], later(2 * i + 1)))

    @pl.when(core == 0)
    def _():
        hand.wait_recv()
        mean_chip, square_chip = joined(
            mean_here, mate[0:1, :], square_here, mate[1:2, :], 2 * CELLS
        )
        st[0, 0:1, :] = mean_chip
        st[0, 1:2, :] = square_chip
        for i in far_first:
            swaps[i + chips - 1].start()
        swaps[0].start()
        for i in far_first:
            swaps[i].start()

    @pl.when(core == 1)
    def _():
        hand.start()

    encode(1)
    send_code(0)
    send_code(1)
    encode(0)
    send_code(2)

    lane = lax.broadcasted_iota(jnp.int32, (8, CHANS), 1)

    def group_sum(row):
        wide = jnp.broadcast_to(row, (8, CHANS))
        for bit in (1, 2, 4):
            wide += jnp.where(
                lane & bit == 0, pltpu.roll(wide, CHANS - bit, 1), pltpu.roll(wide, bit, 1)
            )
        return wide[0:1]

    loads[14].start()
    for copy in loads[5:14]:
        copy.wait()
    ids = lax.broadcasted_iota(jnp.int32, (cams, CHANS), 0)
    my_place = place[cam]
    below_place = place[cam_below]
    below_is_left = below_place == lax.rem(my_place + cams - 1, cams)
    table_row = jnp.sum(jnp.where(ids == my_place, table[...], 0.0), axis=0, keepdims=True)
    extra = jnp.dot(
        jnp.broadcast_to(table_row, (8, CHANS)),
        wq[...].astype(F32),
        precision=lax.Precision.HIGHEST,
        preferred_element_type=F32,
    )[0:1]
    sides = side[...].astype(F32)
    side_below = jnp.where(below_is_left, sides[0:1], sides[1:2])
    side_above = jnp.where(below_is_left, sides[1:2], sides[0:1])
    side_wide = jnp.concatenate(
        [
            jnp.broadcast_to(side_below, (128, CHANS)),
            jnp.broadcast_to(side_above, (128, CHANS)),
        ],
        axis=0,
    ).astype(BF16)

    @pl.when(core == 1)
    def _():
        swaps[0].wait_recv()

    for copy in swaps[1:chips]:
        copy.wait_recv()
    cells = 4 * CELLS
    every = st[:, 0, :]
    mean_chan = jnp.sum(every, axis=0, keepdims=True) / chips
    away = every - mean_chan
    m2_chan = jnp.sum(st[:, 1, :], axis=0, keepdims=True) + cells * jnp.sum(
        away * away, axis=0, keepdims=True
    )
    per_group = CHANS // GROUPS
    mean = group_sum(mean_chan) / per_group
    away = mean_chan - mean
    spread = group_sum(m2_chan + (cells * chips) * (away * away)) / (
        per_group * cells * chips
    )
    scale = lax.rsqrt(spread + 1e-05) * gain[...]
    fw[0:1, :] = mean
    fw[1:2, :] = scale
    forwards = [
        remote(fw, fw_in.at[n], fsend.at[2 * n + i], frecv.at[n], (sides_of[n], t))
        for n in range(2)
        for i, t in enumerate((tm, pair))
    ]

    @pl.when(core == 1)
    def _():
        for copy in forwards:
            copy.start()

    def silu(v):
        h = 0.5 * v
        return (h + h * jnp.tanh(h)).astype(BF16)

    for f in (1, 0):
        hid[half[f], :] = silu((first[half[f], :] - mean) * scale + shift[...])
    for f in (1, 0):
        query[half[f], :] = (dot(hid[half[f], :], wq[...]) + extra).astype(BF16)

    mixed_halo = [
        [
            remote(
                mb.at[2 + f, pl.ds(COLS + at, size)],
                mb.at[f, pl.ds(COLS + at, size)],
                msend.at[2 * f + i],
                mrecv.at[2 * f + i],
                after,
            )
            for i, (at, size) in enumerate(CHUNKS)
        ]
        for f in range(2)
    ]
    tilts = [dot_t(query[half[f], :], side_wide) for f in range(2)]
    for n in range(2):
        forwards[2 * n].wait_recv()

    for f in (1, 0):
        q = query[half[f], :]
        tilt = tilts[f]
        there = []
        for n in range(2):
            for i in (0, 1) if f == 1 else (2,):
                cam_copies[i][n].wait_recv()
            tag = nbr[n, f, pl.ds(CELLS, 16), :].astype(F32)
            scale_there = fw_in[n, 1:2, :]
            factor = tag[12:13] * scale_there
            offset = ((tag[0:1] + tag[8:9]) - fw_in[n, 0:1, :]) * scale_there + shift[...]
            there.append(silu(jnp.log(nbr[n, f, pl.ds(0, CELLS), :].astype(F32)) * factor + offset))
        keys = [dot(rows, wk[...]).astype(BF16) for rows in there]
        values = [dot(rows, wv[...]).astype(BF16) for rows in there]
        attended = []
        for i in range(2):
            part_rows = slice(i * TILE, (i + 1) * TILE)
            bias = [tilt[part_rows, 0:1], tilt[part_rows, 128:129]]
            raw = [dot_t(q[part_rows], keys[n]) for n in range(2)]
            tops = [jnp.max(raw[n], axis=1, keepdims=True) + bias[n] for n in range(2)]
            top = jnp.maximum(tops[0], tops[1])
            expo = [jnp.exp2(raw[n] * SCORE - (top - bias[n]) * SCORE) for n in range(2)]
            total = jnp.sum(expo[0], axis=1, keepdims=True) + jnp.sum(
                expo[1], axis=1, keepdims=True
            )
            inverse = 1.0 / total
            attended.append(
                (
                    dot((expo[0] * inverse).astype(BF16), values[0])
                    + dot((expo[1] * inverse).astype(BF16), values[1])
                ).astype(BF16)
            )
        for i in range(2):
            rows = pl.ds(f * CELLS + i * TILE, TILE)
            mixed = hid[rows, :].astype(F32) + dot(attended[i], wo[...])
            mb[2 + f, pl.ds(COLS + i * TILE, TILE), :] = mixed.astype(BF16)

        @pl.when(jnp.logical_not(is_last))
        def _():
            for copy in mixed_halo[f]:
                copy.start()

    loads[14].wait()
    part[half[0], :] = conv_terms(mb, w2, [(2, 2)])
    part[half[1], :] = conv_terms(mb, w2, [(3, 2), (2, 1)])

    @pl.when(is_first)
    def _():
        mb[0, inner, :] = mb[2, inner, :]
        mb[1, inner, :] = mb[2, inner, :]

    @pl.when(jnp.logical_not(is_first))
    def _():
        for copy in mixed_halo[1]:
            copy.wait_recv()

    total = part[half[1], :] + conv_terms(mb, w2, [(1, 0)])
    out_ref[half[1], :] = (xb[3, inner, :].astype(F32) + total).astype(BF16)
    part[half[0], :] += conv_terms(mb, w2, [(1, 1)])

    for i in range(2):

        @pl.when(jnp.logical_not(is_first))
        def _():
            mixed_halo[0][i].wait_recv()

        rows = pl.ds(i * TILE, TILE)
        total = part[rows, :] + conv_terms(mb, w2, [(0, 0)], i * TILE, TILE)
        out_ref[rows, :] = (xb[2, pl.ds(COLS + i * TILE, TILE), :].astype(F32) + total).astype(BF16)

    for i in range(3):
        for copy in cam_copies[i]:
            copy.wait_send()

    @pl.when(core == 0)
    def _():
        for copy in swaps:
            copy.wait_send()

    @pl.when(core == 1)
    def _():
        hand.wait_send()
        for copy in forwards:
            copy.wait_send()

    @pl.when(jnp.logical_not(is_last))
    def _():
        for copy in halo:
            copy.wait_send()
        for f in range(2):
            for copy in mixed_halo[f]:
                copy.wait_send()


def on_device(
    latents,
    cycle_position,
    conv_first,
    conv_second,
    norm_gain,
    norm_shift,
    w_query,
    w_key,
    w_value,
    w_out,
    camera_table,
    side_embed,
):
    cams, tms = lax.axis_size("cam"), lax.axis_size("tm")
    shape = latents.shape
    vmem = pl.BlockSpec(memory_space=pltpu.VMEM)
    hbm = pl.BlockSpec(memory_space=pltpu.HBM)
    dma = pltpu.SemaphoreType.DMA
    flops = 2 * 1024 * 256 * 256 * (54 + 6) + 4 * 1024 * 1024 * 256
    out = pl.pallas_call(
        functools.partial(block_kernel, cams, tms),
        out_shape=jax.ShapeDtypeStruct((2 * CELLS, CHANS), BF16),
        in_specs=[hbm] * 12,
        out_specs=vmem,
        scratch_shapes=[
            pltpu.VMEM((4, TALL, CHANS), BF16),
            pltpu.VMEM((4, TALL, CHANS), BF16),
            pltpu.VMEM((9, 3 * CHANS, CHANS), BF16),
            pltpu.VMEM((9, 3 * CHANS, CHANS), BF16),
            pltpu.VMEM((2 * CELLS, CHANS), F32),
            pltpu.VMEM((2 * CELLS, CHANS), F32),
            pltpu.VMEM((2, CELLS + 16, CHANS), BF16),
            pltpu.VMEM((2, 2, CELLS + 16, CHANS), BF16),
            pltpu.VMEM((2 * CELLS, CHANS), BF16),
            pltpu.VMEM((2 * CELLS, CHANS), BF16),
            pltpu.VMEM((2, CHANS), F32),
            pltpu.VMEM((2, CHANS), F32),
            pltpu.VMEM((tms // 2, 2, CHANS), F32),
            pltpu.VMEM((2, CHANS), F32),
            pltpu.VMEM((2, 2, CHANS), F32),
            pltpu.SMEM((cams,), jnp.int32),
            pltpu.VMEM((1, CHANS), F32),
            pltpu.VMEM((1, CHANS), F32),
        ]
        + [pltpu.VMEM((CHANS, CHANS), BF16)] * 4
        + [
            pltpu.VMEM((cams, CHANS), F32),
            pltpu.VMEM((2, CHANS), BF16),
            dma((15,)),
            dma((3,)),
            dma((3,)),
            dma((2,)),
            dma((tms,)),
            dma((tms // 2,)),
            dma((6,)),
            dma((6,)),
            dma((4,)),
            dma((2,)),
            dma((4,)),
            dma((4,)),
        ],
        compiler_params=pltpu.CompilerParams(
            collective_id=0, has_side_effects=True, vmem_limit_bytes=62 * 2**20
        ),
        cost_estimate=pl.CostEstimate(
            flops=flops, bytes_accessed=9 * 2**20, transcendentals=2**20
        ),
    )(
        latents.reshape(2 * CELLS, CHANS),
        cycle_position,
        conv_first.reshape(9, 3 * CHANS, CHANS),
        conv_second.reshape(9, 3 * CHANS, CHANS),
        norm_gain.reshape(1, CHANS),
        norm_shift.reshape(1, CHANS),
        w_query,
        w_key,
        w_value,
        w_out,
        camera_table,
        side_embed,
    )
    return out.reshape(shape)


def solution(mesh):
    in_specs = (P("cam", "tm", None, None, None),) + (P(),) * 11
    out_specs = P("cam", "tm", None, None, None)
    return jax.shard_map(
        on_device, mesh=mesh, in_specs=in_specs, out_specs=out_specs, check_vma=False
    )
```
